256 devices in a mesh: dom: 256 (over z, y, x, core).
Axes of the slice: x: 4, y: 4, z: 8, core: 2. Of those that a mesh axis runs over, the one named last changes fastest.
Arguments:
- dofs: float32 [9, 35, 32768], P(None, None, 'dom'), may hold values from -6 to 6
- star: float32 [3, 9, 9, 32768], P(None, None, None, 'dom'), may hold values from -0.8 to 0.8
- flux_local: float32 [4, 9, 9, 32768], P(None, None, None, 'dom'), may hold values from -0.2 to 0.2
- flux_neigh: float32 [4, 9, 9, 32768], P(None, None, None, 'dom'), may hold values from -0.2 to 0.2
- neighbour: int32 [4, 32768], P(None, 'dom'), may hold values from 0 to 32767, as said below
- neighbour_face: int32 [4, 32768], P(None, 'dom'), may hold values from 0 to 3, as said below
- orientation: int32 [4, 32768], P(None, 'dom'), may hold values from 0 to 2, as said below
- face_kind: int32 [4, 32768], P(None, 'dom'), may hold values from 0 to 2
- cluster: int32 [32768], P('dom'), may hold values from 0 to 2, as said below
- deriv_stiff: float32 [3, 35, 35], replicated, may hold values from -1 to 1
- update_stiff: float32 [3, 35, 35], replicated, may hold values from -0.3125 to 0.3125
- face_proj: float32 [4, 15, 35], replicated, may hold values from -1 to 1
- face_lift: float32 [4, 35, 15], replicated, may hold values from -1.5 to 1.5
- orient_map: float32 [3, 15, 15], replicated, may hold values from -1.5 to 1.5
Outputs:
- advanced: float32 [9, 35, 32768], P(None, None, 'dom')
The draws below stay inside these ranges and needn't reach their ends.
Inputs may be any that keep to these rules, and one draw needn't show every extreme that they name: Each partition (a block of 128 consecutive elements) holds exactly 32 elements of cluster 0, 32 of cluster 1 and 64 of cluster 2. The face relation is symmetric: if face f of element e has neighbour n and neighbour_face g, then face g of n has neighbour e and neighbour_face f, with the same orientation. Across an interior face the neighbour lies in the same partition or in a partition one or two apart along the loop of partitions, wrapping at the ends. Two partitions one apart share at most 64 faces and two partitions two apart at most 32; both bounds are reached. A face of kind 1 or 2 names its own element and its own face. `neighbour_face`: see neighbour. `orientation`: equal on both sides of an interior face; 0 on faces of kinds 1 and 2.
All inputs are finite; a program needn't handle non-finite values.
Results may differ from the reference program's by a relative error of at most 0.0003.
Values sent between devices are 32-bit elements; how exact they have to be, the bound alone decides.
A program may use at most 128 MiB of HBM per device.

```python
import math
import jax
import jax.numpy as jnp
from jax import lax

ELEM_DEV = 128
FAST_DEV = 32
MIDDLE_DEV = 32
CAP_NEAR = 64
CAP_FAR = 32
ELEMENTS = 32768
QUANTITIES = 9
BASIS = 35
FACE_BASIS = 15
ORDER = 5
SLOTS = 4
N_DOM = 256


def cluster_table(key):
    places = jnp.arange(ELEM_DEV, dtype=jnp.int32)
    pattern = (places >= FAST_DEV).astype(jnp.int32) + (places >= FAST_DEV + MIDDLE_DEV).astype(jnp.int32)
    part_keys = jax.random.split(jax.random.fold_in(key, 201), N_DOM)
    mixing = jax.vmap(lambda single: jax.random.permutation(single, ELEM_DEV))(part_keys).astype(jnp.int32)
    return jnp.take(pattern, mixing).reshape(-1)


def face_graph(key):
    faces = 4 * ELEM_DEV
    parts = jnp.arange(N_DOM, dtype=jnp.int32)[:, None]
    position = jnp.arange(faces, dtype=jnp.int32)[None, :]
    part_keys = jax.random.split(jax.random.fold_in(key, 101), N_DOM)
    layout = jax.vmap(lambda single: jax.random.permutation(single, faces))(part_keys).astype(jnp.int32)
    near = jax.random.randint(jax.random.fold_in(key, 102), (N_DOM,), CAP_NEAR // 2, CAP_NEAR + 1).at[0].set(CAP_NEAR)
    far = jax.random.randint(jax.random.fold_in(key, 103), (N_DOM,), CAP_FAR // 2, CAP_FAR + 1).at[0].set(CAP_FAR)
    edge_one = near
    edge_two = edge_one + jnp.roll(near, 1)
    edge_three = edge_two + far
    edge_four = edge_three + jnp.roll(far, 2)
    border = ELEM_DEV // 4 + jnp.mod(faces - edge_four - ELEM_DEV // 4, 2)
    edge_five = edge_four + border
    first = edge_one[:, None]
    second = edge_two[:, None]
    third = edge_three[:, None]
    fourth = edge_four[:, None]
    fifth = edge_five[:, None]
    seg_one = position < first
    seg_two = (position >= first) & (position < second)
    seg_three = (position >= second) & (position < third)
    seg_four = (position >= third) & (position < fourth)
    seg_five = (position >= fourth) & (position < fifth)
    seg_start = jnp.where(seg_one, 0, jnp.where(seg_two, first, jnp.where(seg_three, second, jnp.where(seg_four, third, jnp.where(seg_five, fourth, fifth)))))
    within = position - seg_start
    partner_part = jnp.where(seg_one, parts + 1, jnp.where(seg_two, parts - 1, jnp.where(seg_three, parts + 2, jnp.where(seg_four, parts - 2, parts + 0 * position))))
    partner_part = jnp.mod(partner_part, N_DOM).astype(jnp.int32)
    paired_local = fifth + jnp.bitwise_xor(within, 1)
    partner_pos = jnp.where(seg_one, jnp.take(edge_one, partner_part) + within, jnp.where(seg_two, within, jnp.where(seg_three, jnp.take(edge_three, partner_part) + within, jnp.where(seg_four, jnp.take(edge_two, partner_part) + within, jnp.where(seg_five, position + 0 * parts, paired_local)))))
    partner_pos = jnp.clip(partner_pos, 0, faces - 1).astype(jnp.int32)
    partner_slot = layout[partner_part, partner_pos]
    turn_one = jax.random.randint(jax.random.fold_in(key, 104), (N_DOM, faces), 0, 3)
    turn_two = jax.random.randint(jax.random.fold_in(key, 105), (N_DOM, faces), 0, 3)
    turn_local = jax.random.randint(jax.random.fold_in(key, 106), (N_DOM, faces), 0, 3)
    clipped = jnp.clip(within, 0, faces - 1)
    rows_all = parts + 0 * position
    back_one = jnp.mod(rows_all - 1, N_DOM)
    back_two = jnp.mod(rows_all - 2, N_DOM)
    turn = jnp.where(seg_one, turn_one[rows_all, clipped], jnp.where(seg_two, turn_one[back_one, clipped], jnp.where(seg_three, turn_two[rows_all, clipped], jnp.where(seg_four, turn_two[back_two, clipped], jnp.where(seg_five, 0, turn_local[rows_all, clipped // 2])))))
    kinds = jnp.where(seg_five, jax.random.randint(jax.random.fold_in(key, 107), (N_DOM, faces), 1, 3), 0)
    neighbour_value = partner_part * ELEM_DEV + partner_slot // 4
    face_value = jnp.mod(partner_slot, 4)
    inverse = jnp.argsort(layout, axis=1, stable=True).astype(jnp.int32)

    def by_slot(values):
        ordered = jnp.take_along_axis(values.astype(jnp.int32), inverse, axis=1)
        return ordered.reshape(N_DOM, ELEM_DEV, 4).transpose(2, 0, 1).reshape(4, N_DOM * ELEM_DEV)
    return (by_slot(neighbour_value), by_slot(face_value), by_slot(turn), by_slot(kinds))


def draw_cluster(key, part):
    return cluster_table(key)


def draw_neighbour(key, part):
    return face_graph(key)[0]


def draw_neighbour_face(key, part):
    return face_graph(key)[1]


def draw_orientation(key, part):
    return face_graph(key)[2]


def draw_face_kind(key, part):
    return face_graph(key)[3]


def draw_star(key, part):
    factor = jnp.exp2(-cluster_table(key).astype(jnp.float32))
    key = jax.random.fold_in(key, 21)
    shape = (3, QUANTITIES, QUANTITIES, ELEMENTS)
    raw = jax.random.truncated_normal(key, -4.0, 4.0, shape, jnp.float32)
    return 0.2 * raw * factor


def draw_flux_local(key, part):
    factor = jnp.exp2(-cluster_table(key).astype(jnp.float32))
    key = jax.random.fold_in(key, 22)
    shape = (4, QUANTITIES, QUANTITIES, ELEMENTS)
    raw = jax.random.truncated_normal(key, -4.0, 4.0, shape, jnp.float32)
    return 0.05 * raw * factor


def draw_flux_neigh(key, part):
    factor = jnp.exp2(-cluster_table(key).astype(jnp.float32))
    key = jax.random.fold_in(key, 23)
    shape = (4, QUANTITIES, QUANTITIES, ELEMENTS)
    raw = jax.random.truncated_normal(key, -4.0, 4.0, shape, jnp.float32)
    return 0.05 * raw * factor


def steps_of(own_key, dims, cuts, smallest, largest):
    level, own = 1.0, jax.random.fold_in(own_key, 6)
    for dim, blocks in cuts:
        heights = jnp.exp(jax.random.uniform(jax.random.fold_in(own, dim), (blocks,), jnp.float32, smallest / len(cuts), largest / len(cuts)))
        level = level * jnp.repeat(heights, dims[dim] // blocks).reshape([-1 if axis == dim else 1 for axis in range(len(dims))])
    return level


def scatter_about(rng, extent, spread, reach, shards=(), kind=jnp.bfloat16):
    array = jax.random.normal(rng, extent, jnp.float32) * spread
    if len(shards) > 0:
        array = steps_of(rng, extent, shards, -0.22, 0.18) * array
    return jnp.clip(array, min=-reach, max=reach).astype(kind)


def setup_inputs(seed: int = 0) -> dict:
    seeds = jax.random.split(jax.random.key(seed), 15)
    dofs = scatter_about(seeds[0], (QUANTITIES, BASIS, ELEMENTS), 1.0, 6.0, ((2, 256),), jnp.float32)
    star = draw_star(jax.random.fold_in(seeds[14], 71), 0)
    flux_local = draw_flux_local(jax.random.fold_in(seeds[14], 71), 0)
    flux_neigh = draw_flux_neigh(jax.random.fold_in(seeds[14], 71), 0)
    neighbour = draw_neighbour(jax.random.fold_in(seeds[14], 71), 0)
    neighbour_face = draw_neighbour_face(jax.random.fold_in(seeds[14], 71), 0)
    orientation = draw_orientation(jax.random.fold_in(seeds[14], 71), 0)
    face_kind = draw_face_kind(jax.random.fold_in(seeds[14], 71), 0)
    cluster = draw_cluster(jax.random.fold_in(seeds[14], 71), 0)
    deriv_stiff = scatter_about(seeds[9], (3, BASIS, BASIS), BASIS ** -0.5, 1.0, (), jnp.float32)
    update_stiff = scatter_about(seeds[10], (3, BASIS, BASIS), (11 * BASIS) ** -0.5, 0.3125, (), jnp.float32)
    face_proj = scatter_about(seeds[11], (4, FACE_BASIS, BASIS), BASIS ** -0.5, 1.0, (), jnp.float32)
    face_lift = scatter_about(seeds[12], (4, BASIS, FACE_BASIS), FACE_BASIS ** -0.5, 1.5, (), jnp.float32)
    orient_map = scatter_about(seeds[13], (3, FACE_BASIS, FACE_BASIS), FACE_BASIS ** -0.5, 1.5, (), jnp.float32)
    return {"dofs": dofs, "star": star, "flux_local": flux_local, "flux_neigh": flux_neigh, "neighbour": neighbour, "neighbour_face": neighbour_face, "orientation": orientation, "face_kind": face_kind, "cluster": cluster, "deriv_stiff": deriv_stiff, "update_stiff": update_stiff, "face_proj": face_proj, "face_lift": face_lift, "orient_map": orient_map}


HIGHEST = lax.Precision.HIGHEST


def taylor_terms(initial, star, deriv_stiff):
    terms = [initial]
    current = initial
    for degree in range(1, ORDER):
        contracted = jnp.einsum("dxy,pye->dpxe", deriv_stiff, current, precision=HIGHEST)
        current = -jnp.einsum("dqpe,dpxe->qxe", star, contracted, precision=HIGHEST)
        terms.append(current)
    return jnp.stack(terms)


def slot_weights(slot_offset):
    weights_list = []
    for degree in range(ORDER):
        upper = jnp.power(slot_offset + 1.0, degree + 1)
        lower = jnp.power(slot_offset, degree + 1)
        weights_list.append((upper - lower) / math.factorial(degree + 1))
    return jnp.stack(weights_list)


def step_weights(step_span):
    return jnp.stack([jnp.power(step_span, degree + 1) / math.factorial(degree + 1) for degree in range(ORDER)])


def weighted_sum(terms, weights):
    return jnp.sum(terms * weights[:, None, None, :], axis=0)


def update_state(fields, taylor, collected, star, flux_local, flux_neigh, orientation, face_kind, step_span, update_stiff, face_proj, face_lift, orient_map):
    step_integral = weighted_sum(taylor, step_weights(step_span))
    contracted = jnp.einsum("pye,dyx->dpxe", step_integral, update_stiff, precision=HIGHEST)
    volume = jnp.einsum("dqpe,dpxe->qxe", star, contracted, precision=HIGHEST)
    own_faces = jnp.einsum("fmb,qbe->qmfe", face_proj, step_integral, precision=HIGHEST)
    rotated = jnp.zeros_like(collected)
    for rotation in range(3):
        selected = (orientation == rotation).astype(jnp.float32)
        rotated = rotated + selected * jnp.einsum("mn,qnfe->qmfe", orient_map[rotation], collected, precision=HIGHEST)
    mirror_signs = jnp.where(jnp.arange(QUANTITIES) < 6, -1.0, 1.0).astype(jnp.float32)
    mirrored = mirror_signs[:, None, None, None] * own_faces
    outside = jnp.where(face_kind == 0, rotated, jnp.where(face_kind == 1, mirrored, jnp.zeros_like(mirrored)))
    face_terms = jnp.einsum("fqpe,pmfe->qmfe", flux_local, own_faces, precision=HIGHEST)
    face_terms = face_terms + jnp.einsum("fqpe,pmfe->qmfe", flux_neigh, outside, precision=HIGHEST)
    lifted = jnp.einsum("fbm,qmfe->qbe", face_lift, face_terms, precision=HIGHEST)
    return fields + volume - lifted


def reference(dofs, star, flux_local, flux_neigh, neighbour, neighbour_face, orientation, face_kind, cluster, deriv_stiff, update_stiff, face_proj, face_lift, orient_map):
    element_total = dofs.shape[2]
    by_cluster = jnp.argsort(cluster, stable=True).astype(jnp.int32)
    levels = (FAST_DEV * N_DOM, (FAST_DEV + MIDDLE_DEV) * N_DOM, ELEM_DEV * N_DOM)
    span_whole = jnp.left_shift(jnp.ones_like(cluster), cluster).astype(jnp.int32)
    step_span = span_whole.astype(jnp.float32)
    source = (neighbour_face * element_total + neighbour).reshape(-1).astype(jnp.int32)
    fields = dofs
    taylor = jnp.zeros((ORDER,) + dofs.shape, jnp.float32)
    collected = jnp.zeros((QUANTITIES, FACE_BASIS, 4, element_total), jnp.float32)
    for slot_index in range(SLOTS):
        first_level = max(level for level in range(3) if slot_index % (2 ** level) == 0)
        last_level = max(level for level in range(3) if (slot_index + 1) % (2 ** level) == 0)
        starters = by_cluster[:levels[first_level]]
        renewed_terms = taylor_terms(jnp.take(fields, starters, axis=2), jnp.take(star, starters, axis=3), deriv_stiff)
        taylor = taylor.at[:, :, :, starters].set(renewed_terms)
        slot_offset = jnp.mod(slot_index, span_whole).astype(jnp.float32)
        integral = weighted_sum(taylor, slot_weights(slot_offset))
        face_values = jnp.einsum("gmb,qbe->qmge", face_proj, integral, precision=HIGHEST)
        face_values = face_values.reshape(QUANTITIES * FACE_BASIS, 4 * element_total)
        collected = collected + jnp.take(face_values, source, axis=1).reshape(QUANTITIES, FACE_BASIS, 4, element_total)
        finished = by_cluster[:levels[last_level]]
        renewed = update_state(
            jnp.take(fields, finished, axis=2), jnp.take(taylor, finished, axis=3), jnp.take(collected, finished, axis=3),
            jnp.take(star, finished, axis=3), jnp.take(flux_local, finished, axis=3), jnp.take(flux_neigh, finished, axis=3),
            jnp.take(orientation, finished, axis=1), jnp.take(face_kind, finished, axis=1), jnp.take(step_span, finished, axis=0),
            update_stiff, face_proj, face_lift, orient_map)
        fields = fields.at[:, :, finished].set(renewed)
        collected = collected.at[:, :, :, finished].set(0.0)
    return fields
```

```python
import functools

import jax
import jax.numpy as jnp
from jax import lax
from jax.experimental import pallas as pl
from jax.experimental.pallas import tpu as pltpu
from jax.sharding import PartitionSpec as P

ELEM_DEV = 128
CAP_NEAR = 64
CAP_FAR = 32
QUANTITIES = 9
BASIS = 35
FACE_BASIS = 15
ORDER = 5
SLOTS = 4

LANES = 128
ROWS = 40
FROWS = 16
COLS = QUANTITIES * LANES
GROUPS = QUANTITIES * 2
FAR_GROUPS = 5
OFFSETS = (1, -1, 2, -2)
F32 = jnp.float32
BF16 = jnp.bfloat16
HIGHEST = lax.Precision.HIGHEST


def halves(value):
    high = value.astype(BF16).astype(F32)
    return high, value - high


def stacked(value):
    high, low = halves(value)
    tail = jnp.zeros((LANES - 3 * ROWS, value.shape[1]), F32)
    return jnp.concatenate([high, low, high, tail], axis=0).astype(BF16)


def widened(value):
    high, low = halves(value)
    return (high + pltpu.roll(high, ROWS, 1) + pltpu.roll(low, 2 * ROWS, 1)).astype(BF16)


def column_of(row):
    return jnp.broadcast_to(row, (LANES, LANES)).T


def dot(a, b):
    return jnp.dot(a, b, preferred_element_type=F32)


def kernel(
    devices,
    dofs, star, flux_local, flux_neigh, neighbour, neighbour_face, orientation, face_kind, cluster,
    deriv_stiff, update_stiff, face_proj, face_lift, orient_map,
    out,
    fields, start, integral, rhs, product, face_rhs, own_terms, spread, arrived, gathered,
    deriv_w, all_w, lift_w, pad_w, turn_w, tile_w, lift_pad,
    one_local, one_send, one_recv, flux_own,
    near_out, near_in, far_out, far_in, send_sem, recv_sem,
):
    me = lax.axis_index("dom")
    partners = [lax.rem(me + (off + devices), devices) for off in OFFSETS]
    barrier = pltpu.get_barrier_semaphore()
    for partner in partners:
        pl.semaphore_signal(
            barrier, inc=1, device_id=(partner,), device_id_type=pl.DeviceIdType.MESH
        )

    pad_w[...] = jnp.zeros_like(pad_w)
    turn_w[...] = jnp.zeros_like(turn_w)
    tile_w[...] = jnp.zeros_like(tile_w)
    lift_pad[...] = jnp.zeros_like(lift_pad)
    deriv_w[...] = jnp.zeros_like(deriv_w)
    all_w[...] = jnp.zeros_like(all_w)
    for d in range(3):
        pad_w[d * ROWS:d * ROWS + BASIS, 0:BASIS] = deriv_stiff[d]
        tile_w[d, 0:BASIS, 0:BASIS] = update_stiff[d]
    deriv_w[0:128, :] = widened(pad_w[0:128, :])
    for d in range(3):
        pad_w[256 + d * ROWS:256 + (d + 1) * ROWS, :] = tile_w[d].T[0:ROWS, :]
    for f in range(4):
        pad_w[192 + f * FROWS:192 + f * FROWS + FACE_BASIS, :] = jnp.zeros((FACE_BASIS, LANES), F32)
        pad_w[192 + f * FROWS:192 + f * FROWS + FACE_BASIS, 0:BASIS] = face_proj[f]
        lift_pad[f, 0:BASIS, 0:FACE_BASIS] = face_lift[f]
    for o in range(3):
        turn_w[o * FROWS:o * FROWS + FACE_BASIS, 0:FACE_BASIS] = orient_map[o]
    for f in range(4):
        own_rows = pad_w[192 + f * FROWS:192 + (f + 1) * FROWS, :]
        pad_w[f * 48:(f + 1) * 48, :] = jnp.dot(
            turn_w[...], own_rows, precision=HIGHEST, preferred_element_type=F32
        )
    all_w[...] = widened(pad_w[...])
    lift_all = lift_pad[0]
    for f in range(1, 4):
        lift_all = lift_all + pltpu.roll(lift_pad[f], f * FROWS, 1)
    lift_high, lift_low = halves(lift_all)
    lift_w[:, 0:LANES] = (lift_high + pltpu.roll(lift_high, 64, 1)).astype(BF16)
    lift_w[:, LANES:] = lift_low.astype(BF16)

    shape = (4, LANES)
    lane4 = lax.broadcasted_iota(jnp.int32, shape, 1)
    face4 = lax.broadcasted_iota(jnp.int32, shape, 0)
    nb = neighbour[...]
    nf = neighbour_face[...]
    kind = face_kind[...]
    local_id = nb & (ELEM_DEV - 1)
    distance = (nb >> 7) - me
    distance = jnp.where(distance < 0, distance + devices, distance)
    interior = kind == 0
    group = jnp.full(shape, 4, jnp.int32)
    for number, off in enumerate(OFFSETS):
        group = jnp.where(interior & (distance == off % devices), number, group)
    own_key = lane4 * 4 + face4
    far_key = local_id * 4 + nf
    key = jnp.where((group == 0) | (group == 2), own_key, far_key)
    low = (group * 1024).astype(F32)
    full_key = (group * 1024 + key).astype(F32)
    columns = [column_of(full_key[f:f + 1, :]) for f in range(4)]
    ranks = []
    for f in range(4):
        count = jnp.zeros((LANES, LANES), F32)
        for g in range(4):
            before = (columns[g] < full_key[f:f + 1, :]) & (columns[g] >= low[f:f + 1, :])
            count = count + jnp.where(before, 1.0, 0.0)
        ranks.append(jnp.sum(count, axis=0, keepdims=True))
    rank = jnp.concatenate(ranks, axis=0)
    base = jnp.where(group == 0, 0.0, jnp.where(group == 1, 64.0, jnp.where(group == 2, 128.0, 160.0)))
    place = jnp.where(group < 4, base + rank, -1.0)
    inside = interior & (distance == 0)
    source = jnp.where(inside, nf * LANES + local_id, -1).astype(F32)
    row512 = lax.broadcasted_iota(jnp.int32, (4 * LANES, LANES), 0).astype(F32)
    row256 = row512[0:2 * LANES, :]
    lane128 = lax.broadcasted_iota(jnp.int32, (LANES, LANES), 1).astype(F32)
    for f in range(4):
        cols = slice(f * LANES, (f + 1) * LANES)
        one_local[:, cols] = jnp.where(row512 == source[f:f + 1, :], 1.0, 0.0).astype(BF16)
        one_recv[:, cols] = jnp.where(row256 == place[f:f + 1, :], 1.0, 0.0).astype(BF16)
        place_col = column_of(place[f:f + 1, :])
        one_send[cols, 0:LANES] = jnp.where(place_col == lane128, 1.0, 0.0).astype(BF16)
        one_send[cols, LANES:] = jnp.where(place_col == lane128 + 128.0, 1.0, 0.0).astype(BF16)

    mirror = jnp.where(
        lax.broadcasted_iota(jnp.int32, (QUANTITIES, LANES), 0) < 6, -1.0, 1.0
    ).astype(F32)
    for f in range(4):
        factor = mirror * jnp.where(kind[f:f + 1, :] == 1, 1.0, 0.0)
        flux_own[f] = flux_local[f] + factor[None] * flux_neigh[f]

    fields[...] = jnp.zeros_like(fields)
    for q in range(QUANTITIES):
        fields[q, 0:BASIS, :] = dofs[q]
    start[...] = jnp.zeros_like(start)
    face_rhs[...] = jnp.zeros_like(face_rhs)
    pl.semaphore_wait(barrier, 4)

    span_low = jnp.left_shift(jnp.ones((1, LANES), jnp.int32), cluster[...]) - 1
    lane8 = lax.broadcasted_iota(jnp.int32, (8, LANES), 1)
    left = lane8 < 64
    quarter = lane8 // 32
    turned = [orientation[f:f + 1, :] for f in range(4)]

    def col(q):
        return pl.ds(pl.multiple_of(q * LANES, LANES), LANES)

    def contract(row, q_first, count):
        totals = [None] * count
        for d in range(3):
            for p in range(QUANTITIES):
                block = product[row + d * ROWS:row + (d + 1) * ROWS, p * LANES:(p + 1) * LANES]
                for i in range(count):
                    term = star[d, q_first + i, pl.ds(p, 1), :] * block
                    totals[i] = term if totals[i] is None else totals[i] + term
        return totals

    def slot_step(slot, carry):
        offset = span_low & slot
        below = offset.astype(F32)
        above = below + 1.0
        weights = []
        up, down = above, below
        scale = 1.0
        for degree in range(ORDER):
            scale = scale / (degree + 1)
            weights.append((up - down) * scale)
            up, down = up * above, down * below
        begins = offset == 0

        for q in range(QUANTITIES):
            first = jnp.where(begins, fields[q], start[q])
            start[q] = first
            integral[q] = weights[0] * first
            rhs[:, q * LANES:(q + 1) * LANES] = stacked(first)

        for degree in range(1, ORDER):
            product[0:128, :] = dot(deriv_w[...], rhs[...])

            def some(i, c, weight=weights[degree], last=degree == ORDER - 1):
                q_first = i * 3
                totals = contract(0, q_first, 3)
                for j in range(3):
                    q = q_first + j
                    term = -totals[j]
                    total = integral[q] + weight * term
                    if last:
                        rhs[:, col(q)] = stacked(total)
                    else:
                        integral[q] = total
                        rhs[:, col(q)] = stacked(term)
                return c

            lax.fori_loop(0, 3, some, 0)

        product[...] = dot(all_w[...], rhs[...])
        for f in range(4):
            for q in range(QUANTITIES):
                cols = slice(q * LANES, (q + 1) * LANES)
                r = f * 48
                value = jnp.where(
                    turned[f] == 0, product[r:r + 16, cols],
                    jnp.where(turned[f] == 1, product[r + 16:r + 32, cols], product[r + 32:r + 48, cols]),
                )
                high, lower = halves(value)
                spread[q * 16:(q + 1) * 16, f * LANES:(f + 1) * LANES] = high.astype(BF16)
                spread[144 + q * 16:144 + (q + 1) * 16, f * LANES:(f + 1) * LANES] = lower.astype(BF16)

        packed = dot(spread[...], one_send[...])
        packed = packed[0:144, :] + packed[144:288, :]
        near = [packed[r * 8:(r + 1) * 8, 0:LANES] for r in range(GROUPS)]
        far = [packed[r * 8:(r + 1) * 8, LANES:] for r in range(GROUPS)]
        for j in range(QUANTITIES):
            rows = slice(j * 8, (j + 1) * 8)
            near_out[slot, 0, rows, :] = jnp.where(left, near[2 * j], pltpu.roll(near[2 * j + 1], 64, 1))
            near_out[slot, 1, rows, :] = jnp.where(left, pltpu.roll(near[2 * j], 64, 1), near[2 * j + 1])
        for j in range(FAR_GROUPS):
            rows = slice(j * 8, (j + 1) * 8)
            for side in range(2):
                value = pltpu.roll(far[j], (-32 * side) % LANES, 1) if side else far[j]
                for c in range(1, 4):
                    r = j + FAR_GROUPS * c
                    if r < GROUPS:
                        shift = (32 * c - 32 * side) % LANES
                        moved = pltpu.roll(far[r], shift, 1) if shift else far[r]
                        value = jnp.where(quarter == c, moved, value)
                far_out[slot, side, rows, :] = value

        copies = []
        for number in range(4):
            here, there = (near_out, near_in) if number < 2 else (far_out, far_in)
            copies.append(pltpu.make_async_remote_copy(
                src_ref=here.at[slot, number % 2],
                dst_ref=there.at[slot, 1 - number % 2],
                send_sem=send_sem.at[slot, number],
                recv_sem=recv_sem.at[slot, number ^ 1],
                device_id=(partners[number],),
                device_id_type=pl.DeviceIdType.MESH,
            ))
        for copy in copies:
            copy.start()

        def volume(i, c):
            totals = contract(256, i * 3, 3)
            for j in range(3):
                fields[i * 3 + j] = fields[i * 3 + j] + totals[j]
            return c

        lax.fori_loop(0, 3, volume, 0)

        def own_part(f, c):
            row = pl.multiple_of(f * FROWS, FROWS)
            values = [product[pl.ds(pl.multiple_of(192 + row, FROWS), FROWS), p * LANES:(p + 1) * LANES]
                      for p in range(QUANTITIES)]
            for q in range(QUANTITIES):
                total = None
                for p in range(QUANTITIES):
                    term = flux_own[f, q, pl.ds(p, 1), :] * values[p]
                    total = term if total is None else total + term
                own_terms[pl.ds(row, FROWS), q * LANES:(q + 1) * LANES] = total
            return c

        lax.fori_loop(0, 4, own_part, 0)
        both = dot(spread[...], one_local[...])
        gathered[...] = both[0:144, :] + both[144:288, :]

        for number in range(4):
            copies[number].wait_recv()
        for j in range(QUANTITIES):
            rows = slice(j * 8, (j + 1) * 8)
            ahead, behind = near_in[slot, 0, rows, :], near_in[slot, 1, rows, :]
            even = jnp.where(left, ahead, pltpu.roll(behind, 64, 1))
            odd = jnp.where(left, pltpu.roll(ahead, 64, 1), behind)
            high, lower = halves(jnp.concatenate([even, odd], axis=0))
            arrived[j * 16:(j + 1) * 16, 0:LANES] = high.astype(BF16)
            arrived[144 + j * 16:144 + (j + 1) * 16, 0:LANES] = lower.astype(BF16)
        pieces = [None] * GROUPS
        for j in range(FAR_GROUPS):
            rows = slice(j * 8, (j + 1) * 8)
            ahead, behind = far_in[slot, 0, rows, :], far_in[slot, 1, rows, :]
            for c in range(4):
                r = j + FAR_GROUPS * c
                if r < GROUPS:
                    first = pltpu.roll(ahead, (-32 * c) % LANES, 1) if c else ahead
                    shift = (32 - 32 * c) % LANES
                    second = pltpu.roll(behind, shift, 1) if shift else behind
                    pieces[r] = jnp.where(quarter == 0, first, second)
        for j in range(QUANTITIES):
            high, lower = halves(jnp.concatenate([pieces[2 * j], pieces[2 * j + 1]], axis=0))
            arrived[j * 16:(j + 1) * 16, LANES:] = high.astype(BF16)
            arrived[144 + j * 16:144 + (j + 1) * 16, LANES:] = lower.astype(BF16)
        both = dot(arrived[...], one_recv[...])
        gathered[...] = gathered[...] + (both[0:144, :] + both[144:288, :])

        def outside_part(f, c):
            row = pl.multiple_of(f * FROWS, FROWS)
            values = [gathered[p * FROWS:(p + 1) * FROWS, col(f)] for p in range(QUANTITIES)]
            for q in range(QUANTITIES):
                cols = slice(q * LANES, (q + 1) * LANES)
                total = own_terms[pl.ds(row, FROWS), cols]
                for p in range(QUANTITIES):
                    total = total + flux_neigh[f, q, pl.ds(p, 1), :] * values[p]
                high, lower = halves(total)
                high = high.astype(BF16)
                face_rhs[pl.ds(row, FROWS), cols] = high
                face_rhs[pl.ds(pl.multiple_of(row + 64, FROWS), FROWS), cols] = lower.astype(BF16)
                face_rhs[pl.ds(pl.multiple_of(row + 128, FROWS), FROWS), cols] = high
            return c

        lax.fori_loop(0, 4, outside_part, 0)
        lifted = dot(lift_w[...], face_rhs[...])
        for q in range(QUANTITIES):
            fields[q] = fields[q] - lifted[0:ROWS, q * LANES:(q + 1) * LANES]
        for copy in copies:
            copy.wait_send()
        return carry

    lax.fori_loop(0, SLOTS, slot_step, 0)
    for q in range(QUANTITIES):
        out[q] = fields[q, 0:BASIS, :]


def body(devices, *args):
    args = list(args)
    args[8] = args[8].reshape(1, -1)
    vmem = pl.BlockSpec(memory_space=pltpu.VMEM)
    scratch = [
        pltpu.VMEM((QUANTITIES, ROWS, LANES), F32),
        pltpu.VMEM((QUANTITIES, ROWS, LANES), F32),
        pltpu.VMEM((QUANTITIES, ROWS, LANES), F32),
        pltpu.VMEM((LANES, COLS), BF16),
        pltpu.VMEM((384, COLS), F32),
        pltpu.VMEM((256, COLS), BF16),
        pltpu.VMEM((4 * FROWS, COLS), F32),
        pltpu.VMEM((288, 512), BF16),
        pltpu.VMEM((288, 256), BF16),
        pltpu.VMEM((144, 512), F32),
        pltpu.VMEM((128, LANES), BF16),
        pltpu.VMEM((384, LANES), BF16),
        pltpu.VMEM((ROWS, 2 * LANES), BF16),
        pltpu.VMEM((384, LANES), F32),
        pltpu.VMEM((48, FROWS), F32),
        pltpu.VMEM((3, LANES, LANES), F32),
        pltpu.VMEM((4, ROWS, LANES), F32),
        pltpu.VMEM((512, 512), BF16),
        pltpu.VMEM((512, 256), BF16),
        pltpu.VMEM((256, 512), BF16),
        pltpu.VMEM((4, QUANTITIES, QUANTITIES, LANES), F32),
        pltpu.VMEM((SLOTS, 2, QUANTITIES * 8, LANES), F32),
        pltpu.VMEM((SLOTS, 2, QUANTITIES * 8, LANES), F32),
        pltpu.VMEM((SLOTS, 2, FAR_GROUPS * 8, LANES), F32),
        pltpu.VMEM((SLOTS, 2, FAR_GROUPS * 8, LANES), F32),
        pltpu.SemaphoreType.DMA((SLOTS, 4)),
        pltpu.SemaphoreType.DMA((SLOTS, 4)),
    ]
    return pl.pallas_call(
        functools.partial(kernel, devices),
        out_shape=jax.ShapeDtypeStruct(args[0].shape, F32),
        in_specs=[vmem] * len(args),
        out_specs=vmem,
        scratch_shapes=scratch,
        compiler_params=pltpu.CompilerParams(
            collective_id=0, has_side_effects=True, vmem_limit_bytes=40 * 2**20
        ),
    )(*args)


def solution(mesh):
    in_specs = (
        P(None, None, "dom"),
        P(None, None, None, "dom"),
        P(None, None, None, "dom"),
        P(None, None, None, "dom"),
        P(None, "dom"),
        P(None, "dom"),
        P(None, "dom"),
        P(None, "dom"),
        P("dom"),
        P(),
        P(),
        P(),
        P(),
        P(),
    )
    return jax.shard_map(
        functools.partial(body, mesh.shape["dom"]),
        mesh=mesh, in_specs=in_specs, out_specs=P(None, None, "dom"), check_vma=False,
    )
```

```python
import functools

import jax
import jax.numpy as jnp
from jax import lax
from jax.experimental import pallas as pl
from jax.experimental.pallas import tpu as pltpu
from jax.sharding import PartitionSpec as P

ELEM_DEV = 128
CAP_NEAR = 64
CAP_FAR = 32
QUANTITIES = 9
BASIS = 35
FACE_BASIS = 15
ORDER = 5
SLOTS = 4

LANES = 128
ROWS = 40
FROWS = 16
COLS = QUANTITIES * LANES
GROUPS = QUANTITIES * 2
FAR_GROUPS = 5
OFFSETS = (1, -1, 2, -2)
F32 = jnp.float32
BF16 = jnp.bfloat16
HIGHEST = lax.Precision.HIGHEST


def halves(value):
    high = value.astype(BF16).astype(F32)
    return high, value - high


def stacked(value):
    high, low = halves(value)
    tail = jnp.zeros((LANES - 3 * ROWS, value.shape[1]), F32)
    return jnp.concatenate([high, low, high, tail], axis=0).astype(BF16)


def widened(value):
    high, low = halves(value)
    return (high + pltpu.roll(high, ROWS, 1) + pltpu.roll(low, 2 * ROWS, 1)).astype(BF16)


def column_of(row):
    return jnp.broadcast_to(row, (LANES, LANES)).T


def dot(a, b):
    return jnp.dot(a, b, preferred_element_type=F32)


def kernel(devices, *refs):
    operands, out, landed, (
        fields, start, integral, rhs, product, face_rhs, own_terms, spread, arrived, gathered,
        deriv_w, all_w, lift_w, pad_w, turn_w, tile_w,
        one_local, one_send, one_recv, where_from, flux_own,
        near_out, near_in, far_out, far_in, send_sem, recv_sem,
        in_sem,
    ) = refs[:14], refs[14], refs[15:29], refs[29:]
    (
        dofs, star, flux_local, flux_neigh, neighbour, neighbour_face, orientation, face_kind, cluster,
        deriv_stiff, update_stiff, face_proj, face_lift, orient_map,
    ) = landed
    loads = [
        pltpu.make_async_copy(operands[number], landed[number], in_sem.at[number])
        for number in range(14)
    ]
    first_loads = (4, 5, 7, 11, 13, 9, 10)
    then_loads = (8, 0, 1)
    late_loads = (6, 12, 2, 3)
    for number in first_loads + then_loads + late_loads:
        loads[number].start()

    me = lax.axis_index("dom")
    partners = [lax.rem(me + (off + devices), devices) for off in OFFSETS]
    barrier = pltpu.get_barrier_semaphore()
    for partner in partners:
        pl.semaphore_signal(
            barrier, inc=1, device_id=(partner,), device_id_type=pl.DeviceIdType.MESH
        )

    pad_w[...] = jnp.zeros_like(pad_w)
    turn_w[...] = jnp.zeros_like(turn_w)
    tile_w[...] = jnp.zeros_like(tile_w)
    deriv_w[...] = jnp.zeros_like(deriv_w)
    all_w[...] = jnp.zeros_like(all_w)
    fields[...] = jnp.zeros_like(fields)
    start[...] = jnp.zeros_like(start)
    face_rhs[...] = jnp.zeros_like(face_rhs)
    for number in first_loads:
        loads[number].wait()
    for d in range(3):
        pad_w[d * ROWS:d * ROWS + BASIS, 0:BASIS] = deriv_stiff[d]
        tile_w[d, 0:BASIS, 0:BASIS] = update_stiff[d]
    deriv_w[0:128, :] = widened(pad_w[0:128, :])
    for d in range(3):
        pad_w[256 + d * ROWS:256 + (d + 1) * ROWS, :] = tile_w[d].T[0:ROWS, :]
    for f in range(4):
        pad_w[192 + f * FROWS:192 + (f + 1) * FROWS, :] = jnp.zeros((FROWS, LANES), F32)
        pad_w[192 + f * FROWS:192 + f * FROWS + FACE_BASIS, 0:BASIS] = face_proj[:, f, :]
    for o in range(3):
        turn_w[o * FROWS:o * FROWS + FACE_BASIS, 0:FACE_BASIS] = orient_map[o]
    own_rows = jnp.concatenate(
        [pad_w[192 + f * FROWS:192 + (f + 1) * FROWS, :] for f in range(4)], axis=1
    )
    turned_rows = jnp.dot(turn_w[...], own_rows, precision=HIGHEST, preferred_element_type=F32)
    for f in range(4):
        pad_w[f * 48:(f + 1) * 48, :] = turned_rows[:, f * LANES:(f + 1) * LANES]
    all_w[...] = widened(pad_w[...])

    shape = (4, LANES)
    lane4 = lax.broadcasted_iota(jnp.int32, shape, 1)
    face4 = lax.broadcasted_iota(jnp.int32, shape, 0)
    nb = neighbour[...]
    nf = neighbour_face[...]
    kind = face_kind[...]
    local_id = nb & (ELEM_DEV - 1)
    distance = (nb >> 7) - me
    distance = jnp.where(distance < 0, distance + devices, distance)
    interior = kind == 0
    group = jnp.full(shape, 4, jnp.int32)
    for number, off in enumerate(OFFSETS):
        group = jnp.where(interior & (distance == off % devices), number, group)
    own_key = lane4 * 4 + face4
    far_key = local_id * 4 + nf
    key = jnp.where((group == 0) | (group == 2), own_key, far_key)
    low = (group * 1024).astype(F32)
    full_key = (group * 1024 + key).astype(F32)
    columns = [column_of(full_key[f:f + 1, :]) for f in range(4)]
    ranks = []
    for f in range(4):
        count = jnp.zeros((LANES, LANES), F32)
        for g in range(4):
            before = (columns[g] < full_key[f:f + 1, :]) & (columns[g] >= low[f:f + 1, :])
            count = count + jnp.where(before, 1.0, 0.0)
        ranks.append(jnp.sum(count, axis=0, keepdims=True))
    rank = jnp.concatenate(ranks, axis=0)
    base = jnp.where(group == 0, 0.0, jnp.where(group == 1, 64.0, jnp.where(group == 2, 128.0, 160.0)))
    place = jnp.where(group < 4, base + rank, -1.0)
    inside = interior & (distance == 0)
    source = jnp.where(inside, nf * LANES + local_id, -1).astype(F32)
    lane128 = lax.broadcasted_iota(jnp.int32, (LANES, LANES), 1).astype(F32)
    for f in range(4):
        cols = slice(f * LANES, (f + 1) * LANES)
        place_col = column_of(place[f:f + 1, :])
        one_send[cols, 0:LANES] = jnp.where(place_col == lane128, 1.0, 0.0).astype(BF16)
        one_send[cols, LANES:] = jnp.where(place_col == lane128 + 128.0, 1.0, 0.0).astype(BF16)
    where_from[0] = source
    where_from[1] = place

    def late_setup():
        row512 = lax.broadcasted_iota(jnp.int32, (4 * LANES, LANES), 0).astype(F32)
        row256 = row512[0:2 * LANES, :]
        for f in range(4):
            cols = slice(f * LANES, (f + 1) * LANES)
            one_local[:, cols] = jnp.where(row512 == where_from[0, f:f + 1, :], 1.0, 0.0).astype(BF16)
            one_recv[:, cols] = jnp.where(row256 == where_from[1, f:f + 1, :], 1.0, 0.0).astype(BF16)
        mirror = jnp.where(
            lax.broadcasted_iota(jnp.int32, (QUANTITIES, 4, LANES), 0) < 6, -1.0, 1.0
        ).astype(F32)
        factor = mirror * jnp.where(face_kind[...] == 1, 1.0, 0.0)[None]
        for q in range(QUANTITIES):
            flux_own[q] = flux_local[q] + factor * flux_neigh[q]
        for f in range(4):
            tile_w[3, f * FROWS:f * FROWS + FACE_BASIS, 0:BASIS] = face_lift[:, f, :]
        lift_high, lift_low = halves(tile_w[3].T[0:ROWS, :])
        lift_w[:, 0:LANES] = (lift_high + pltpu.roll(lift_high, 64, 1)).astype(BF16)
        lift_w[:, LANES:] = lift_low.astype(BF16)

    for number in then_loads + late_loads:
        loads[number].wait()
    for q in range(QUANTITIES):
        fields[q, 0:BASIS, :] = dofs[q]
    pl.semaphore_wait(barrier, 4)

    span_low = jnp.left_shift(jnp.ones((1, LANES), jnp.int32), cluster[...]) - 1
    lane8 = lax.broadcasted_iota(jnp.int32, (8, LANES), 1)
    left = lane8 < 64
    quarter = lane8 // 32
    turned = [orientation[f:f + 1, :] for f in range(4)]

    def col(q):
        return pl.ds(pl.multiple_of(q * LANES, LANES), LANES)

    def contract(row, q_first, count):
        totals = [None] * count
        for d in range(3):
            for p in range(QUANTITIES):
                block = product[row + d * ROWS:row + (d + 1) * ROWS, p * LANES:(p + 1) * LANES]
                for i in range(count):
                    term = star[q_first + i, p, d:d + 1, :] * block
                    totals[i] = term if totals[i] is None else totals[i] + term
        return totals

    def slot_step(slot, carry):
        offset = span_low & slot
        below = offset.astype(F32)
        above = below + 1.0
        weights = []
        up, down = above, below
        scale = 1.0
        for degree in range(ORDER):
            scale = scale / (degree + 1)
            weights.append((up - down) * scale)
            up, down = up * above, down * below
        begins = offset == 0

        for q in range(QUANTITIES):
            first = jnp.where(begins, fields[q], start[q])
            start[q] = first
            integral[q] = weights[0] * first
            rhs[:, q * LANES:(q + 1) * LANES] = stacked(first)

        for degree in range(1, ORDER):
            product[0:128, :] = dot(deriv_w[...], rhs[...])

            def some(i, c, weight=weights[degree], last=degree == ORDER - 1):
                q_first = i * 3
                totals = contract(0, q_first, 3)
                for j in range(3):
                    q = q_first + j
                    term = -totals[j]
                    total = integral[q] + weight * term
                    if last:
                        rhs[:, col(q)] = stacked(total)
                    else:
                        integral[q] = total
                        rhs[:, col(q)] = stacked(term)
                return c

            lax.fori_loop(0, 3, some, 0)

        product[...] = dot(all_w[...], rhs[...])
        for f in range(4):
            for q in range(QUANTITIES):
                cols = slice(q * LANES, (q + 1) * LANES)
                r = f * 48
                value = jnp.where(
                    turned[f] == 0, product[r:r + 16, cols],
                    jnp.where(turned[f] == 1, product[r + 16:r + 32, cols], product[r + 32:r + 48, cols]),
                )
                high, lower = halves(value)
                spread[q * 16:(q + 1) * 16, f * LANES:(f + 1) * LANES] = high.astype(BF16)
                spread[144 + q * 16:144 + (q + 1) * 16, f * LANES:(f + 1) * LANES] = lower.astype(BF16)

        packed = dot(spread[...], one_send[...])
        packed = packed[0:144, :] + packed[144:288, :]
        near = [packed[r * 8:(r + 1) * 8, 0:LANES] for r in range(GROUPS)]
        far = [packed[r * 8:(r + 1) * 8, LANES:] for r in range(GROUPS)]
        for j in range(QUANTITIES):
            rows = slice(j * 8, (j + 1) * 8)
            near_out[slot, 0, rows, :] = jnp.where(left, near[2 * j], pltpu.roll(near[2 * j + 1], 64, 1))
            near_out[slot, 1, rows, :] = jnp.where(left, pltpu.roll(near[2 * j], 64, 1), near[2 * j + 1])
        for j in range(FAR_GROUPS):
            rows = slice(j * 8, (j + 1) * 8)
            for side in range(2):
                value = pltpu.roll(far[j], (-32 * side) % LANES, 1) if side else far[j]
                for c in range(1, 4):
                    r = j + FAR_GROUPS * c
                    if r < GROUPS:
                        shift = (32 * c - 32 * side) % LANES
                        moved = pltpu.roll(far[r], shift, 1) if shift else far[r]
                        value = jnp.where(quarter == c, moved, value)
                far_out[slot, side, rows, :] = value

        copies = []
        for number in range(4):
            here, there = (near_out, near_in) if number < 2 else (far_out, far_in)
            copies.append(pltpu.make_async_remote_copy(
                src_ref=here.at[slot, number % 2],
                dst_ref=there.at[slot, 1 - number % 2],
                send_sem=send_sem.at[slot, number],
                recv_sem=recv_sem.at[slot, number ^ 1],
                device_id=(partners[number],),
                device_id_type=pl.DeviceIdType.MESH,
            ))
        for copy in copies:
            copy.start()

        pl.when(slot == 0)(late_setup)
        def volume(i, c):
            totals = contract(256, i * 3, 3)
            for j in range(3):
                fields[i * 3 + j] = fields[i * 3 + j] + totals[j]
            return c

        lax.fori_loop(0, 3, volume, 0)

        def own_part(f, c):
            row = pl.multiple_of(f * FROWS, FROWS)
            values = [product[pl.ds(pl.multiple_of(192 + row, FROWS), FROWS), p * LANES:(p + 1) * LANES]
                      for p in range(QUANTITIES)]
            for q in range(QUANTITIES):
                total = None
                for p in range(QUANTITIES):
                    term = flux_own[q, p, pl.ds(f, 1), :] * values[p]
                    total = term if total is None else total + term
                own_terms[pl.ds(row, FROWS), q * LANES:(q + 1) * LANES] = total
            return c

        lax.fori_loop(0, 4, own_part, 0)
        both = dot(spread[...], one_local[...])
        gathered[...] = both[0:144, :] + both[144:288, :]

        for number in range(4):
            copies[number].wait_recv()
        for j in range(QUANTITIES):
            rows = slice(j * 8, (j + 1) * 8)
            ahead, behind = near_in[slot, 0, rows, :], near_in[slot, 1, rows, :]
            even = jnp.where(left, ahead, pltpu.roll(behind, 64, 1))
            odd = jnp.where(left, pltpu.roll(ahead, 64, 1), behind)
            high, lower = halves(jnp.concatenate([even, odd], axis=0))
            arrived[j * 16:(j + 1) * 16, 0:LANES] = high.astype(BF16)
            arrived[144 + j * 16:144 + (j + 1) * 16, 0:LANES] = lower.astype(BF16)
        pieces = [None] * GROUPS
        for j in range(FAR_GROUPS):
            rows = slice(j * 8, (j + 1) * 8)
            ahead, behind = far_in[slot, 0, rows, :], far_in[slot, 1, rows, :]
            for c in range(4):
                r = j + FAR_GROUPS * c
                if r < GROUPS:
                    first = pltpu.roll(ahead, (-32 * c) % LANES, 1) if c else ahead
                    shift = (32 - 32 * c) % LANES
                    second = pltpu.roll(behind, shift, 1) if shift else behind
                    pieces[r] = jnp.where(quarter == 0, first, second)
        for j in range(QUANTITIES):
            high, lower = halves(jnp.concatenate([pieces[2 * j], pieces[2 * j + 1]], axis=0))
            arrived[j * 16:(j + 1) * 16, LANES:] = high.astype(BF16)
            arrived[144 + j * 16:144 + (j + 1) * 16, LANES:] = lower.astype(BF16)
        both = dot(arrived[...], one_recv[...])
        gathered[...] = gathered[...] + (both[0:144, :] + both[144:288, :])

        def outside_part(f, c):
            row = pl.multiple_of(f * FROWS, FROWS)
            values = [gathered[p * FROWS:(p + 1) * FROWS, col(f)] for p in range(QUANTITIES)]
            for q in range(QUANTITIES):
                cols = slice(q * LANES, (q + 1) * LANES)
                total = own_terms[pl.ds(row, FROWS), cols]
                for p in range(QUANTITIES):
                    total = total + flux_neigh[q, p, pl.ds(f, 1), :] * values[p]
                high, lower = halves(total)
                high = high.astype(BF16)
                face_rhs[pl.ds(row, FROWS), cols] = high
                face_rhs[pl.ds(pl.multiple_of(row + 64, FROWS), FROWS), cols] = lower.astype(BF16)
                face_rhs[pl.ds(pl.multiple_of(row + 128, FROWS), FROWS), cols] = high
            return c

        lax.fori_loop(0, 4, outside_part, 0)
        lifted = dot(lift_w[...], face_rhs[...])
        for q in range(QUANTITIES):
            fields[q] = fields[q] - lifted[0:ROWS, q * LANES:(q + 1) * LANES]
        for copy in copies:
            copy.wait_send()
        return carry

    lax.fori_loop(0, SLOTS, slot_step, 0)
    for q in range(QUANTITIES):
        out[q] = fields[q, 0:BASIS, :]


def body(devices, *args):
    args = list(args)
    args[8] = args[8].reshape(1, -1)
    for number in (1, 2, 3):
        args[number] = jnp.transpose(args[number], (1, 2, 0, 3))
    args[11] = jnp.transpose(args[11], (1, 0, 2))
    args[12] = jnp.transpose(args[12], (2, 0, 1))
    vmem = pl.BlockSpec(memory_space=pltpu.VMEM)
    hbm = pl.BlockSpec(memory_space=pltpu.HBM)
    scratch = [pltpu.VMEM(arg.shape, arg.dtype) for arg in args] + [
        pltpu.VMEM((QUANTITIES, ROWS, LANES), F32),
        pltpu.VMEM((QUANTITIES, ROWS, LANES), F32),
        pltpu.VMEM((QUANTITIES, ROWS, LANES), F32),
        pltpu.VMEM((LANES, COLS), BF16),
        pltpu.VMEM((384, COLS), F32),
        pltpu.VMEM((256, COLS), BF16),
        pltpu.VMEM((4 * FROWS, COLS), F32),
        pltpu.VMEM((288, 512), BF16),
        pltpu.VMEM((288, 256), BF16),
        pltpu.VMEM((144, 512), F32),
        pltpu.VMEM((128, LANES), BF16),
        pltpu.VMEM((384, LANES), BF16),
        pltpu.VMEM((ROWS, 2 * LANES), BF16),
        pltpu.VMEM((384, LANES), F32),
        pltpu.VMEM((48, FROWS), F32),
        pltpu.VMEM((4, LANES, LANES), F32),
        pltpu.VMEM((512, 512), BF16),
        pltpu.VMEM((512, 256), BF16),
        pltpu.VMEM((256, 512), BF16),
        pltpu.VMEM((2, 4, LANES), F32),
        pltpu.VMEM((QUANTITIES, QUANTITIES, 4, LANES), F32),
        pltpu.VMEM((SLOTS, 2, QUANTITIES * 8, LANES), F32),
        pltpu.VMEM((SLOTS, 2, QUANTITIES * 8, LANES), F32),
        pltpu.VMEM((SLOTS, 2, FAR_GROUPS * 8, LANES), F32),
        pltpu.VMEM((SLOTS, 2, FAR_GROUPS * 8, LANES), F32),
        pltpu.SemaphoreType.DMA((SLOTS, 4)),
        pltpu.SemaphoreType.DMA((SLOTS, 4)),
        pltpu.SemaphoreType.DMA((14,)),
    ]
    args = [pltpu.with_memory_space_constraint(arg, pltpu.HBM) for arg in args]
    return pl.pallas_call(
        functools.partial(kernel, devices),
        out_shape=jax.ShapeDtypeStruct(args[0].shape, F32),
        in_specs=[hbm] * len(args),
        out_specs=vmem,
        scratch_shapes=scratch,
        compiler_params=pltpu.CompilerParams(
            collective_id=0, has_side_effects=True, vmem_limit_bytes=40 * 2**20
        ),
    )(*args)


def solution(mesh):
    in_specs = (
        P(None, None, "dom"),
        P(None, None, None, "dom"),
        P(None, None, None, "dom"),
        P(None, None, None, "dom"),
        P(None, "dom"),
        P(None, "dom"),
        P(None, "dom"),
        P(None, "dom"),
        P("dom"),
        P(),
        P(),
        P(),
        P(),
        P(),
    )
    return jax.shard_map(
        functools.partial(body, mesh.shape["dom"]),
        mesh=mesh, in_specs=in_specs, out_specs=P(None, None, "dom"), check_vma=False,
    )
```

```python
import functools

import jax
import jax.numpy as jnp
from jax import lax
from jax.experimental import pallas as pl
from jax.experimental.pallas import tpu as pltpu
from jax.sharding import PartitionSpec as P

ELEM_DEV = 128
CAP_NEAR = 64
CAP_FAR = 32
QUANTITIES = 9
BASIS = 35
FACE_BASIS = 15
ORDER = 5
SLOTS = 4

LANES = 128
ROWS = 40
FROWS = 16
COLS = QUANTITIES * LANES
GROUPS = QUANTITIES * 2
FAR_GROUPS = 5
OFFSETS = (1, -1, 2, -2)
F32 = jnp.float32
BF16 = jnp.bfloat16
HIGHEST = lax.Precision.HIGHEST


def halves(value):
    high = value.astype(BF16).astype(F32)
    return high, value - high


def stacked(value):
    high, low = halves(value)
    tail = jnp.zeros((LANES - 3 * ROWS, value.shape[1]), F32)
    return jnp.concatenate([high, low, high, tail], axis=0).astype(BF16)


def widened(value):
    high, low = halves(value)
    return (high + pltpu.roll(high, ROWS, 1) + pltpu.roll(low, 2 * ROWS, 1)).astype(BF16)


def column_of(row):
    return jnp.broadcast_to(row, (LANES, LANES)).T


def dot(a, b):
    return jnp.dot(a, b, preferred_element_type=F32)


def kernel(devices, *refs):
    operands, out, landed, (
        fields, start, integral, rhs, product, face_rhs, own_terms, spread, arrived, gathered,
        deriv_w, all_w, lift_w, pad_w, turn_w, tile_w,
        one_local, one_send, one_recv, where_from, flux_own,
        near_out, near_in, far_out, far_in, send_sem, recv_sem,
        in_sem,
    ) = refs[:14], refs[14], refs[15:29], refs[29:]
    (
        dofs, star, flux_local, flux_neigh, neighbour, neighbour_face, orientation, face_kind, cluster,
        deriv_stiff, update_stiff, face_proj, face_lift, orient_map,
    ) = landed
    loads = [
        pltpu.make_async_copy(operands[number], landed[number], in_sem.at[number])
        for number in range(14)
    ]
    first_loads = (4, 5, 7, 11, 13, 9, 10)
    then_loads = (8, 0, 1)
    late_loads = (6, 12, 2, 3)
    for number in first_loads + then_loads + late_loads:
        loads[number].start()

    me = lax.axis_index("dom")
    partners = [lax.rem(me + (off + devices), devices) for off in OFFSETS]
    barrier = pltpu.get_barrier_semaphore()
    for partner in partners:
        pl.semaphore_signal(
            barrier, inc=1, device_id=(partner,), device_id_type=pl.DeviceIdType.MESH
        )

    pad_w[...] = jnp.zeros_like(pad_w)
    turn_w[...] = jnp.zeros_like(turn_w)
    tile_w[...] = jnp.zeros_like(tile_w)
    deriv_w[...] = jnp.zeros_like(deriv_w)
    all_w[...] = jnp.zeros_like(all_w)
    fields[...] = jnp.zeros_like(fields)
    start[...] = jnp.zeros_like(start)
    face_rhs[...] = jnp.zeros_like(face_rhs)
    for number in first_loads:
        loads[number].wait()
    for d in range(3):
        pad_w[d * ROWS:d * ROWS + BASIS, 0:BASIS] = deriv_stiff[d]
        tile_w[d, 0:BASIS, 0:BASIS] = update_stiff[d]
    deriv_w[0:128, :] = widened(pad_w[0:128, :])
    for d in range(3):
        pad_w[256 + d * ROWS:256 + (d + 1) * ROWS, :] = tile_w[d].T[0:ROWS, :]
    for f in range(4):
        pad_w[192 + f * FROWS:192 + (f + 1) * FROWS, :] = jnp.zeros((FROWS, LANES), F32)
        pad_w[192 + f * FROWS:192 + f * FROWS + FACE_BASIS, 0:BASIS] = face_proj[:, f, :]
    for o in range(3):
        turn_w[o * FROWS:o * FROWS + FACE_BASIS, 0:FACE_BASIS] = orient_map[o]
    own_rows = jnp.concatenate(
        [pad_w[192 + f * FROWS:192 + (f + 1) * FROWS, :] for f in range(4)], axis=1
    )
    turned_rows = jnp.dot(turn_w[...], own_rows, precision=HIGHEST, preferred_element_type=F32)
    for f in range(4):
        pad_w[f * 48:(f + 1) * 48, :] = turned_rows[:, f * LANES:(f + 1) * LANES]
    all_w[...] = widened(pad_w[...])

    shape = (4, LANES)
    lane4 = lax.broadcasted_iota(jnp.int32, shape, 1)
    face4 = lax.broadcasted_iota(jnp.int32, shape, 0)
    nb = neighbour[...]
    nf = neighbour_face[...]
    kind = face_kind[...]
    local_id = nb & (ELEM_DEV - 1)
    distance = (nb >> 7) - me
    distance = jnp.where(distance < 0, distance + devices, distance)
    interior = kind == 0
    group = jnp.full(shape, 4, jnp.int32)
    for number, off in enumerate(OFFSETS):
        group = jnp.where(interior & (distance == off % devices), number, group)
    own_key = lane4 * 4 + face4
    far_key = local_id * 4 + nf
    key = jnp.where((group == 0) | (group == 2), own_key, far_key)
    low = (group * 1024).astype(F32)
    full_key = (group * 1024 + key).astype(F32)
    columns = [column_of(full_key[f:f + 1, :]) for f in range(4)]
    ranks = []
    for f in range(4):
        count = jnp.zeros((LANES, LANES), F32)
        for g in range(4):
            before = (columns[g] < full_key[f:f + 1, :]) & (columns[g] >= low[f:f + 1, :])
            count = count + jnp.where(before, 1.0, 0.0)
        ranks.append(jnp.sum(count, axis=0, keepdims=True))
    rank = jnp.concatenate(ranks, axis=0)
    base = jnp.where(group == 0, 0.0, jnp.where(group == 1, 64.0, jnp.where(group == 2, 128.0, 160.0)))
    place = jnp.where(group < 4, base + rank, -1.0)
    inside = interior & (distance == 0)
    source = jnp.where(inside, nf * LANES + local_id, -1).astype(F32)
    lane128 = lax.broadcasted_iota(jnp.int32, (LANES, LANES), 1).astype(F32)
    for f in range(4):
        cols = slice(f * LANES, (f + 1) * LANES)
        place_col = column_of(place[f:f + 1, :])
        one_send[cols, 0:LANES] = jnp.where(place_col == lane128, 1.0, 0.0).astype(BF16)
        one_send[cols, LANES:] = jnp.where(place_col == lane128 + 128.0, 1.0, 0.0).astype(BF16)
    where_from[0] = source
    where_from[1] = place

    def late_setup():
        row512 = lax.broadcasted_iota(jnp.int32, (4 * LANES, LANES), 0).astype(F32)
        row256 = row512[0:2 * LANES, :]
        for f in range(4):
            cols = slice(f * LANES, (f + 1) * LANES)
            one_local[:, cols] = jnp.where(row512 == where_from[0, f:f + 1, :], 1.0, 0.0).astype(BF16)
            one_recv[:, cols] = jnp.where(row256 == where_from[1, f:f + 1, :], 1.0, 0.0).astype(BF16)
        mirror = jnp.where(
            lax.broadcasted_iota(jnp.int32, (QUANTITIES, 4, LANES), 0) < 6, -1.0, 1.0
        ).astype(F32)
        factor = mirror * jnp.where(face_kind[...] == 1, 1.0, 0.0)[None]
        for q in range(QUANTITIES):
            flux_own[q] = flux_local[q] + factor * flux_neigh[q]
        for f in range(4):
            tile_w[3, f * FROWS:f * FROWS + FACE_BASIS, 0:BASIS] = face_lift[:, f, :]
        lift_high, lift_low = halves(tile_w[3].T[0:ROWS, :])
        lift_w[:, 0:LANES] = (lift_high + pltpu.roll(lift_high, 64, 1)).astype(BF16)
        lift_w[:, LANES:] = lift_low.astype(BF16)

    for number in then_loads + late_loads:
        loads[number].wait()
    for q in range(QUANTITIES):
        fields[q, 0:BASIS, :] = dofs[q]
    pl.semaphore_wait(barrier, 4)

    span_low = jnp.left_shift(jnp.ones((1, LANES), jnp.int32), cluster[...]) - 1
    lane8 = lax.broadcasted_iota(jnp.int32, (8, LANES), 1)
    left = lane8 < 64
    quarter = lane8 // 32
    turned = [orientation[f:f + 1, :] for f in range(4)]

    def col(q):
        return pl.ds(q * LANES, LANES)

    def contract(row, q_first, count):
        totals = [None] * count
        for p in range(QUANTITIES):
            for d in range(3):
                block = product[row + d * ROWS:row + (d + 1) * ROWS, p * LANES:(p + 1) * LANES]
                for i in range(count):
                    term = star[q_first + i, p, d:d + 1, :] * block
                    totals[i] = term if totals[i] is None else totals[i] + term
        return totals

    def slot_step(slot, carry):
        offset = span_low & slot
        below = offset.astype(F32)
        above = below + 1.0
        weights = []
        up, down = above, below
        scale = 1.0
        for degree in range(ORDER):
            scale = scale / (degree + 1)
            weights.append((up - down) * scale)
            up, down = up * above, down * below
        begins = offset == 0

        for q in range(QUANTITIES):
            first = jnp.where(begins, fields[q], start[q])
            start[q] = first
            integral[q] = weights[0] * first
            rhs[:, q * LANES:(q + 1) * LANES] = stacked(first)

        for degree in range(1, ORDER):
            for tile in range(0, COLS, 256):
                stop = min(tile + 256, COLS)
                product[0:128, tile:stop] = dot(deriv_w[...], rhs[:, tile:stop])

            def some(i, c, weight=weights[degree], last=degree == ORDER - 1):
                q_first = i * 3
                totals = contract(0, q_first, 3)
                for j in range(3):
                    q = q_first + j
                    term = -totals[j]
                    total = integral[q] + weight * term
                    if last:
                        rhs[:, col(q)] = stacked(total)
                    else:
                        integral[q] = total
                        rhs[:, col(q)] = stacked(term)
                return c

            for block in range(3):
                some(block, 0)

        product[...] = dot(all_w[...], rhs[...])
        for f in range(4):
            for q in range(QUANTITIES):
                cols = slice(q * LANES, (q + 1) * LANES)
                r = f * 48
                value = jnp.where(
                    turned[f] == 0, product[r:r + 16, cols],
                    jnp.where(turned[f] == 1, product[r + 16:r + 32, cols], product[r + 32:r + 48, cols]),
                )
                high, lower = halves(value)
                spread[q * 16:(q + 1) * 16, f * LANES:(f + 1) * LANES] = high.astype(BF16)
                spread[144 + q * 16:144 + (q + 1) * 16, f * LANES:(f + 1) * LANES] = lower.astype(BF16)

        packed = dot(spread[...], one_send[...])
        packed = packed[0:144, :] + packed[144:288, :]
        near = [packed[r * 8:(r + 1) * 8, 0:LANES] for r in range(GROUPS)]
        far = [packed[r * 8:(r + 1) * 8, LANES:] for r in range(GROUPS)]
        for j in range(QUANTITIES):
            rows = slice(j * 8, (j + 1) * 8)
            near_out[slot, 0, rows, :] = jnp.where(left, near[2 * j], pltpu.roll(near[2 * j + 1], 64, 1))
            near_out[slot, 1, rows, :] = jnp.where(left, pltpu.roll(near[2 * j], 64, 1), near[2 * j + 1])
        for j in range(FAR_GROUPS):
            rows = slice(j * 8, (j + 1) * 8)
            for side in range(2):
                value = pltpu.roll(far[j], (-32 * side) % LANES, 1) if side else far[j]
                for c in range(1, 4):
                    r = j + FAR_GROUPS * c
                    if r < GROUPS:
                        shift = (32 * c - 32 * side) % LANES
                        moved = pltpu.roll(far[r], shift, 1) if shift else far[r]
                        value = jnp.where(quarter == c, moved, value)
                far_out[slot, side, rows, :] = value

        copies = []
        for number in range(4):
            here, there = (near_out, near_in) if number < 2 else (far_out, far_in)
            copies.append(pltpu.make_async_remote_copy(
                src_ref=here.at[slot, number % 2],
                dst_ref=there.at[slot, 1 - number % 2],
                send_sem=send_sem.at[slot, number],
                recv_sem=recv_sem.at[slot, number ^ 1],
                device_id=(partners[number],),
                device_id_type=pl.DeviceIdType.MESH,
            ))
        for copy in copies:
            copy.start()

        pl.when(slot == 0)(late_setup)
        def volume(i, c):
            totals = contract(256, i * 3, 3)
            for j in range(3):
                fields[i * 3 + j] = fields[i * 3 + j] + totals[j]
            return c

        for block in range(3):
            volume(block, 0)

        def own_part(f, c):
            row = f * FROWS
            values = [product[pl.ds(192 + row, FROWS), p * LANES:(p + 1) * LANES]
                      for p in range(QUANTITIES)]
            for q in range(QUANTITIES):
                total = None
                for p in range(QUANTITIES):
                    term = flux_own[q, p, pl.ds(f, 1), :] * values[p]
                    total = term if total is None else total + term
                own_terms[pl.ds(row, FROWS), q * LANES:(q + 1) * LANES] = total
            return c

        for block in range(4):
            own_part(block, 0)
        both = dot(spread[...], one_local[...])
        gathered[...] = both[0:144, :] + both[144:288, :]

        for number in range(4):
            copies[number].wait_recv()
        for j in range(QUANTITIES):
            rows = slice(j * 8, (j + 1) * 8)
            ahead, behind = near_in[slot, 0, rows, :], near_in[slot, 1, rows, :]
            even = jnp.where(left, ahead, pltpu.roll(behind, 64, 1))
            odd = jnp.where(left, pltpu.roll(ahead, 64, 1), behind)
            high, lower = halves(jnp.concatenate([even, odd], axis=0))
            arrived[j * 16:(j + 1) * 16, 0:LANES] = high.astype(BF16)
            arrived[144 + j * 16:144 + (j + 1) * 16, 0:LANES] = lower.astype(BF16)
        pieces = [None] * GROUPS
        for j in range(FAR_GROUPS):
            rows = slice(j * 8, (j + 1) * 8)
            ahead, behind = far_in[slot, 0, rows, :], far_in[slot, 1, rows, :]
            for c in range(4):
                r = j + FAR_GROUPS * c
                if r < GROUPS:
                    first = pltpu.roll(ahead, (-32 * c) % LANES, 1) if c else ahead
                    shift = (32 - 32 * c) % LANES
                    second = pltpu.roll(behind, shift, 1) if shift else behind
                    pieces[r] = jnp.where(quarter == 0, first, second)
        for j in range(QUANTITIES):
            high, lower = halves(jnp.concatenate([pieces[2 * j], pieces[2 * j + 1]], axis=0))
            arrived[j * 16:(j + 1) * 16, LANES:] = high.astype(BF16)
            arrived[144 + j * 16:144 + (j + 1) * 16, LANES:] = lower.astype(BF16)
        both = dot(arrived[...], one_recv[...])
        gathered[...] = gathered[...] + (both[0:144, :] + both[144:288, :])

        def outside_part(f, c):
            row = f * FROWS
            values = [gathered[p * FROWS:(p + 1) * FROWS, col(f)] for p in range(QUANTITIES)]
            for q in range(QUANTITIES):
                cols = slice(q * LANES, (q + 1) * LANES)
                total = own_terms[pl.ds(row, FROWS), cols]
                for p in range(QUANTITIES):
                    total = total + flux_neigh[q, p, pl.ds(f, 1), :] * values[p]
                high, lower = halves(total)
                high = high.astype(BF16)
                face_rhs[pl.ds(row, FROWS), cols] = high
                face_rhs[pl.ds(row + 64, FROWS), cols] = lower.astype(BF16)
                face_rhs[pl.ds(row + 128, FROWS), cols] = high
            return c

        for block in range(4):
            outside_part(block, 0)
        lifted = dot(lift_w[...], face_rhs[...])
        for q in range(QUANTITIES):
            fields[q] = fields[q] - lifted[0:ROWS, q * LANES:(q + 1) * LANES]
        for copy in copies:
            copy.wait_send()
        return carry

    lax.fori_loop(0, SLOTS, slot_step, 0)
    for q in range(QUANTITIES):
        out[q] = fields[q, 0:BASIS, :]


def body(devices, *args):
    args = list(args)
    args[8] = args[8].reshape(1, -1)
    for number in (1, 2, 3):
        args[number] = jnp.transpose(args[number], (1, 2, 0, 3))
    args[11] = jnp.transpose(args[11], (1, 0, 2))
    args[12] = jnp.transpose(args[12], (2, 0, 1))
    vmem = pl.BlockSpec(memory_space=pltpu.VMEM)
    hbm = pl.BlockSpec(memory_space=pltpu.HBM)
    scratch = [pltpu.VMEM(arg.shape, arg.dtype) for arg in args] + [
        pltpu.VMEM((QUANTITIES, ROWS, LANES), F32),
        pltpu.VMEM((QUANTITIES, ROWS, LANES), F32),
        pltpu.VMEM((QUANTITIES, ROWS, LANES), F32),
        pltpu.VMEM((LANES, COLS), BF16),
        pltpu.VMEM((384, COLS), F32),
        pltpu.VMEM((256, COLS), BF16),
        pltpu.VMEM((4 * FROWS, COLS), F32),
        pltpu.VMEM((288, 512), BF16),
        pltpu.VMEM((288, 256), BF16),
        pltpu.VMEM((144, 512), F32),
        pltpu.VMEM((128, LANES), BF16),
        pltpu.VMEM((384, LANES), BF16),
        pltpu.VMEM((ROWS, 2 * LANES), BF16),
        pltpu.VMEM((384, LANES), F32),
        pltpu.VMEM((48, FROWS), F32),
        pltpu.VMEM((4, LANES, LANES), F32),
        pltpu.VMEM((512, 512), BF16),
        pltpu.VMEM((512, 256), BF16),
        pltpu.VMEM((256, 512), BF16),
        pltpu.VMEM((2, 4, LANES), F32),
        pltpu.VMEM((QUANTITIES, QUANTITIES, 4, LANES), F32),
        pltpu.VMEM((SLOTS, 2, QUANTITIES * 8, LANES), F32),
        pltpu.VMEM((SLOTS, 2, QUANTITIES * 8, LANES), F32),
        pltpu.VMEM((SLOTS, 2, FAR_GROUPS * 8, LANES), F32),
        pltpu.VMEM((SLOTS, 2, FAR_GROUPS * 8, LANES), F32),
        pltpu.SemaphoreType.DMA((SLOTS, 4)),
        pltpu.SemaphoreType.DMA((SLOTS, 4)),
        pltpu.SemaphoreType.DMA((14,)),
    ]
    args = [pltpu.with_memory_space_constraint(arg, pltpu.HBM) for arg in args]
    return pl.pallas_call(
        functools.partial(kernel, devices),
        out_shape=jax.ShapeDtypeStruct(args[0].shape, F32),
        in_specs=[hbm] * len(args),
        out_specs=vmem,
        scratch_shapes=scratch,
        compiler_params=pltpu.CompilerParams(
            collective_id=0, has_side_effects=True, vmem_limit_bytes=40 * 2**20
        ),
    )(*args)


def solution(mesh):
    in_specs = (
        P(None, None, "dom"),
        P(None, None, None, "dom"),
        P(None, None, None, "dom"),
        P(None, None, None, "dom"),
        P(None, "dom"),
        P(None, "dom"),
        P(None, "dom"),
        P(None, "dom"),
        P("dom"),
        P(),
        P(),
        P(),
        P(),
        P(),
    )
    return jax.shard_map(
        functools.partial(body, mesh.shape["dom"]),
        mesh=mesh, in_specs=in_specs, out_specs=P(None, None, "dom"), check_vma=False,
    )
```

```python
import functools

import jax
import jax.numpy as jnp
from jax import lax
from jax.experimental import pallas as pl
from jax.experimental.pallas import tpu as pltpu
from jax.sharding import PartitionSpec as P

ELEM_DEV = 128
CAP_NEAR = 64
CAP_FAR = 32
QUANTITIES = 9
BASIS = 35
FACE_BASIS = 15
ORDER = 5
SLOTS = 4

LANES = 128
ROWS = 40
FROWS = 16
COLS = QUANTITIES * LANES
GROUPS = QUANTITIES * 2
FAR_GROUPS = 5
OFFSETS = (1, -1, 2, -2)
BLOCKS = ((0, 1, 2, 3), (4, 5, 6, 7), (8,))
F32 = jnp.float32
BF16 = jnp.bfloat16
HIGHEST = lax.Precision.HIGHEST


def halves(value):
    high = value.astype(BF16).astype(F32)
    return high, value - high


def stacked(value):
    high, low = halves(value)
    tail = jnp.zeros((LANES - 3 * ROWS, value.shape[1]), F32)
    return jnp.concatenate([high, low, high, tail], axis=0).astype(BF16)


def widened(value):
    high, low = halves(value)
    return (high + pltpu.roll(high, ROWS, 1) + pltpu.roll(low, 2 * ROWS, 1)).astype(BF16)


def column_of(row):
    return jnp.broadcast_to(row, (LANES, LANES)).T


def dot(a, b):
    return jnp.dot(a, b, preferred_element_type=F32)


def kernel(devices, *refs):
    operands, out, landed, (
        fields, start, integral, rhs, first_z, second_z, turned_out, own_out, face_rhs, own_terms, spread, arrived, gathered,
        deriv_w, all_w, lift_w, pad_w, turn_w, tile_w,
        one_local, one_send, one_recv, where_from, flux_own,
        near_out, near_in, far_out, far_in, send_sem, recv_sem,
        in_sem,
    ) = refs[:14], refs[14], refs[15:29], refs[29:]
    (
        dofs, star, flux_local, flux_neigh, neighbour, neighbour_face, orientation, face_kind, cluster,
        deriv_stiff, update_stiff, face_proj, face_lift, orient_map,
    ) = landed
    loads = [
        pltpu.make_async_copy(operands[number], landed[number], in_sem.at[number])
        for number in range(14)
    ]
    first_loads = (9, 0, 1, 8, 4, 5, 7, 11, 13, 10, 6)
    late_loads = (12, 2, 3)
    for number in first_loads + late_loads:
        loads[number].start()

    me = lax.axis_index("dom")
    partners = [lax.rem(me + (off + devices), devices) for off in OFFSETS]
    barrier = pltpu.get_barrier_semaphore()
    for partner in partners:
        pl.semaphore_signal(
            barrier, inc=1, device_id=(partner,), device_id_type=pl.DeviceIdType.MESH
        )

    pad_w[...] = jnp.zeros_like(pad_w)
    turn_w[...] = jnp.zeros_like(turn_w)
    tile_w[...] = jnp.zeros_like(tile_w)
    deriv_w[...] = jnp.zeros_like(deriv_w)
    all_w[...] = jnp.zeros_like(all_w)
    fields[...] = jnp.zeros_like(fields)
    start[...] = jnp.zeros_like(start)
    face_rhs[...] = jnp.zeros_like(face_rhs)
    for number in first_loads:
        loads[number].wait()
    for d in range(3):
        pad_w[d * ROWS:d * ROWS + BASIS, 0:BASIS] = deriv_stiff[d]
        tile_w[d, 0:BASIS, 0:BASIS] = update_stiff[d]
    deriv_w[0:128, :] = widened(pad_w[0:128, :])
    for d in range(3):
        pad_w[256 + d * ROWS:256 + (d + 1) * ROWS, :] = tile_w[d].T[0:ROWS, :]
    for f in range(4):
        pad_w[192 + f * FROWS:192 + (f + 1) * FROWS, :] = jnp.zeros((FROWS, LANES), F32)
        pad_w[192 + f * FROWS:192 + f * FROWS + FACE_BASIS, 0:BASIS] = face_proj[:, f, :]
    for o in range(3):
        turn_w[o * FROWS:o * FROWS + FACE_BASIS, 0:FACE_BASIS] = orient_map[o]
    own_rows = jnp.concatenate(
        [pad_w[192 + f * FROWS:192 + (f + 1) * FROWS, :] for f in range(4)], axis=1
    )
    turned_rows = jnp.dot(turn_w[...], own_rows, precision=HIGHEST, preferred_element_type=F32)
    for f in range(4):
        pad_w[f * 48:(f + 1) * 48, :] = turned_rows[:, f * LANES:(f + 1) * LANES]
    all_w[...] = widened(pad_w[...])

    shape = (4, LANES)
    lane4 = lax.broadcasted_iota(jnp.int32, shape, 1)
    face4 = lax.broadcasted_iota(jnp.int32, shape, 0)
    nb = neighbour[...]
    nf = neighbour_face[...]
    kind = face_kind[...]
    local_id = nb & (ELEM_DEV - 1)
    distance = (nb >> 7) - me
    distance = jnp.where(distance < 0, distance + devices, distance)
    interior = kind == 0
    group = jnp.full(shape, 4, jnp.int32)
    for number, off in enumerate(OFFSETS):
        group = jnp.where(interior & (distance == off % devices), number, group)
    own_key = lane4 * 4 + face4
    far_key = local_id * 4 + nf
    key = jnp.where((group == 0) | (group == 2), own_key, far_key)
    low = (group * 1024).astype(F32)
    full_key = (group * 1024 + key).astype(F32)
    columns = [column_of(full_key[f:f + 1, :]) for f in range(4)]
    ranks = []
    for f in range(4):
        count = jnp.zeros((LANES, LANES), F32)
        for g in range(4):
            before = (columns[g] < full_key[f:f + 1, :]) & (columns[g] >= low[f:f + 1, :])
            count = count + jnp.where(before, 1.0, 0.0)
        ranks.append(jnp.sum(count, axis=0, keepdims=True))
    rank = jnp.concatenate(ranks, axis=0)
    base = jnp.where(group == 0, 0.0, jnp.where(group == 1, 64.0, jnp.where(group == 2, 128.0, 160.0)))
    place = jnp.where(group < 4, base + rank, -1.0)
    inside = interior & (distance == 0)
    source = jnp.where(inside, nf * LANES + local_id, -1).astype(F32)
    lane128 = lax.broadcasted_iota(jnp.int32, (LANES, LANES), 1).astype(F32)
    for f in range(4):
        cols = slice(f * LANES, (f + 1) * LANES)
        place_col = column_of(place[f:f + 1, :])
        one_send[cols, 0:LANES] = jnp.where(place_col == lane128, 1.0, 0.0).astype(BF16)
        one_send[cols, LANES:] = jnp.where(place_col == lane128 + 128.0, 1.0, 0.0).astype(BF16)
    where_from[0] = source
    where_from[1] = place

    def late_setup():
        for number in late_loads:
            loads[number].wait()
        row512 = lax.broadcasted_iota(jnp.int32, (4 * LANES, LANES), 0).astype(F32)
        row256 = row512[0:2 * LANES, :]
        for f in range(4):
            cols = slice(f * LANES, (f + 1) * LANES)
            one_local[:, cols] = jnp.where(row512 == where_from[0, f:f + 1, :], 1.0, 0.0).astype(BF16)
            one_recv[:, cols] = jnp.where(row256 == where_from[1, f:f + 1, :], 1.0, 0.0).astype(BF16)
        mirror = jnp.where(
            lax.broadcasted_iota(jnp.int32, (QUANTITIES, 4, LANES), 0) < 6, -1.0, 1.0
        ).astype(F32)
        factor = mirror * jnp.where(face_kind[...] == 1, 1.0, 0.0)[None]
        for q in range(QUANTITIES):
            flux_own[q] = flux_local[q] + factor * flux_neigh[q]
        for f in range(4):
            tile_w[3, f * FROWS:f * FROWS + FACE_BASIS, 0:BASIS] = face_lift[:, f, :]
        lift_high, lift_low = halves(tile_w[3].T[0:ROWS, :])
        lift_w[:, 0:LANES] = (lift_high + pltpu.roll(lift_high, 64, 1)).astype(BF16)
        lift_w[:, LANES:] = lift_low.astype(BF16)

    for q in range(QUANTITIES):
        fields[q, 0:BASIS, :] = dofs[q]

    span_low = jnp.left_shift(jnp.ones((1, LANES), jnp.int32), cluster[...]) - 1
    lane8 = lax.broadcasted_iota(jnp.int32, (8, LANES), 1)
    left = lane8 < 64
    quarter = lane8 // 32
    turned = [orientation[f:f + 1, :] for f in range(4)]

    def span_of(block):
        return slice(block[0] * LANES, (block[-1] + 1) * LANES)

    def col(q):
        return slice(q * LANES, (q + 1) * LANES)

    def contract(source_ref, row, block):
        totals = [None] * len(block)
        for p in range(QUANTITIES):
            for d in range(3):
                values = source_ref[row + d * ROWS:row + (d + 1) * ROWS, col(p)]
                for i, q in enumerate(block):
                    term = star[q, p, d:d + 1, :] * values
                    totals[i] = term if totals[i] is None else totals[i] + term
        return totals

    def face_contract(flux, source_ref, f, block, where):
        totals = [None] * len(block)
        for p in range(QUANTITIES):
            values = source_ref[where(f, p)]
            for i, q in enumerate(block):
                term = flux[q, p, f:f + 1, :] * values
                totals[i] = term if totals[i] is None else totals[i] + term
        return totals

    def slot_step(slot, carry, first_slot=False):
        offset = span_low & slot
        below = offset.astype(F32)
        above = below + 1.0
        weights = []
        up, down = above, below
        scale = 1.0
        for degree in range(ORDER):
            scale = scale / (degree + 1)
            weights.append((up - down) * scale)
            up, down = up * above, down * below
        begins = offset == 0

        for block in BLOCKS:
            for q in block:
                first = fields[q] if first_slot else jnp.where(begins, fields[q], start[q])
                start[q] = first
                integral[q] = weights[0] * first
                rhs[:, col(q)] = stacked(first)
            first_z[:, span_of(block)] = dot(deriv_w[...], rhs[:, span_of(block)])

        packed = []
        for degree in range(1, ORDER):
            z_now, z_next = (first_z, second_z) if degree % 2 else (second_z, first_z)
            last = degree == ORDER - 1
            for block in BLOCKS:
                totals = contract(z_now, 0, block)
                for q, total in zip(block, totals):
                    term = -total
                    sum_now = integral[q] + weights[degree] * term
                    if last:
                        rhs[:, col(q)] = stacked(sum_now)
                    else:
                        integral[q] = sum_now
                        rhs[:, col(q)] = stacked(term)
                cols = span_of(block)
                if last:
                    turned_out[:, cols] = dot(all_w[0:192, :], rhs[:, cols])
                    for q in block:
                        for f in range(4):
                            r = f * 48
                            value = jnp.where(
                                turned[f] == 0, turned_out[r:r + 16, col(q)],
                                jnp.where(turned[f] == 1, turned_out[r + 16:r + 32, col(q)],
                                          turned_out[r + 32:r + 48, col(q)]),
                            )
                            high, lower = halves(value)
                            spread[q * 32:q * 32 + 16, col(f)] = high.astype(BF16)
                            spread[q * 32 + 16:q * 32 + 32, col(f)] = lower.astype(BF16)
                    piece = dot(spread[block[0] * 32:(block[-1] + 1) * 32, :], one_send[...])
                    for i in range(len(block)):
                        packed.append(piece[i * 32:i * 32 + 16, :] + piece[i * 32 + 16:i * 32 + 32, :])
                else:
                    z_next[:, cols] = dot(deriv_w[...], rhs[:, cols])

        packed = jnp.concatenate(packed, axis=0)
        near = [packed[r * 8:(r + 1) * 8, 0:LANES] for r in range(GROUPS)]
        far = [packed[r * 8:(r + 1) * 8, LANES:] for r in range(GROUPS)]
        for j in range(QUANTITIES):
            rows = slice(j * 8, (j + 1) * 8)
            near_out[slot, 0, rows, :] = jnp.where(left, near[2 * j], pltpu.roll(near[2 * j + 1], 64, 1))
            near_out[slot, 1, rows, :] = jnp.where(left, pltpu.roll(near[2 * j], 64, 1), near[2 * j + 1])
        for j in range(FAR_GROUPS):
            rows = slice(j * 8, (j + 1) * 8)
            for side in range(2):
                value = pltpu.roll(far[j], (-32 * side) % LANES, 1) if side else far[j]
                for c in range(1, 4):
                    r = j + FAR_GROUPS * c
                    if r < GROUPS:
                        shift = (32 * c - 32 * side) % LANES
                        moved = pltpu.roll(far[r], shift, 1) if shift else far[r]
                        value = jnp.where(quarter == c, moved, value)
                far_out[slot, side, rows, :] = value

        if first_slot:
            pl.semaphore_wait(barrier, 4)
        copies = []
        for number in range(4):
            here, there = (near_out, near_in) if number < 2 else (far_out, far_in)
            copies.append(pltpu.make_async_remote_copy(
                src_ref=here.at[slot, number % 2],
                dst_ref=there.at[slot, 1 - number % 2],
                send_sem=send_sem.at[slot, number],
                recv_sem=recv_sem.at[slot, number ^ 1],
                device_id=(partners[number],),
                device_id_type=pl.DeviceIdType.MESH,
            ))
        for copy in copies:
            copy.start()

        if first_slot:
            late_setup()
        both = dot(spread[...], one_local[...])
        for q in range(QUANTITIES):
            gathered[q * 16:q * 16 + 16, :] = both[q * 32:q * 32 + 16, :] + both[q * 32 + 16:q * 32 + 32, :]
        for block in BLOCKS:
            own_out[:, span_of(block)] = dot(all_w[192:384, :], rhs[:, span_of(block)])
        for block in BLOCKS:
            totals = contract(own_out, 64, block)
            for q, total in zip(block, totals):
                fields[q] = fields[q] + total
        for f in range(4):
            for block in BLOCKS:
                totals = face_contract(
                    flux_own, own_out, f, block, lambda f, p: (slice(f * FROWS, (f + 1) * FROWS), col(p))
                )
                for q, total in zip(block, totals):
                    own_terms[f * FROWS:(f + 1) * FROWS, col(q)] = total

        for number in range(4):
            copies[number].wait_recv()
        for j in range(QUANTITIES):
            rows = slice(j * 8, (j + 1) * 8)
            ahead, behind = near_in[slot, 0, rows, :], near_in[slot, 1, rows, :]
            even = jnp.where(left, ahead, pltpu.roll(behind, 64, 1))
            odd = jnp.where(left, pltpu.roll(ahead, 64, 1), behind)
            high, lower = halves(jnp.concatenate([even, odd], axis=0))
            arrived[j * 16:(j + 1) * 16, 0:LANES] = high.astype(BF16)
            arrived[144 + j * 16:144 + (j + 1) * 16, 0:LANES] = lower.astype(BF16)
        pieces = [None] * GROUPS
        for j in range(FAR_GROUPS):
            rows = slice(j * 8, (j + 1) * 8)
            ahead, behind = far_in[slot, 0, rows, :], far_in[slot, 1, rows, :]
            for c in range(4):
                r = j + FAR_GROUPS * c
                if r < GROUPS:
                    first = pltpu.roll(ahead, (-32 * c) % LANES, 1) if c else ahead
                    shift = (32 - 32 * c) % LANES
                    second = pltpu.roll(behind, shift, 1) if shift else behind
                    pieces[r] = jnp.where(quarter == 0, first, second)
        for j in range(QUANTITIES):
            high, lower = halves(jnp.concatenate([pieces[2 * j], pieces[2 * j + 1]], axis=0))
            arrived[j * 16:(j + 1) * 16, LANES:] = high.astype(BF16)
            arrived[144 + j * 16:144 + (j + 1) * 16, LANES:] = lower.astype(BF16)
        both = dot(arrived[...], one_recv[...])
        gathered[...] = gathered[...] + (both[0:144, :] + both[144:288, :])

        for block in BLOCKS:
            cols = span_of(block)
            for f in range(4):
                totals = face_contract(
                    flux_neigh, gathered, f, block, lambda f, p: (slice(p * FROWS, (p + 1) * FROWS), col(f))
                )
                for q, total in zip(block, totals):
                    row = f * FROWS
                    high, lower = halves(own_terms[row:row + FROWS, col(q)] + total)
                    high = high.astype(BF16)
                    face_rhs[row:row + FROWS, col(q)] = high
                    face_rhs[row + 64:row + 64 + FROWS, col(q)] = lower.astype(BF16)
                    face_rhs[row + 128:row + 128 + FROWS, col(q)] = high
            lifted = dot(lift_w[...], face_rhs[:, cols])
            for i, q in enumerate(block):
                fields[q] = fields[q] - lifted[0:ROWS, col(i)]
        for copy in copies:
            copy.wait_send()
        return carry

    slot_step(0, 0, first_slot=True)
    lax.fori_loop(1, SLOTS, slot_step, 0)
    for q in range(QUANTITIES):
        out[q] = fields[q, 0:BASIS, :]


def body(devices, *args):
    args = list(args)
    args[8] = args[8].reshape(1, -1)
    for number in (1, 2, 3):
        args[number] = jnp.transpose(args[number], (1, 2, 0, 3))
    args[11] = jnp.transpose(args[11], (1, 0, 2))
    args[12] = jnp.transpose(args[12], (2, 0, 1))
    vmem = pl.BlockSpec(memory_space=pltpu.VMEM)
    hbm = pl.BlockSpec(memory_space=pltpu.HBM)
    scratch = [pltpu.VMEM(arg.shape, arg.dtype) for arg in args] + [
        pltpu.VMEM((QUANTITIES, ROWS, LANES), F32),
        pltpu.VMEM((QUANTITIES, ROWS, LANES), F32),
        pltpu.VMEM((QUANTITIES, ROWS, LANES), F32),
        pltpu.VMEM((LANES, COLS), BF16),
        pltpu.VMEM((128, COLS), F32),
        pltpu.VMEM((128, COLS), F32),
        pltpu.VMEM((192, COLS), F32),
        pltpu.VMEM((192, COLS), F32),
        pltpu.VMEM((256, COLS), BF16),
        pltpu.VMEM((4 * FROWS, COLS), F32),
        pltpu.VMEM((288, 512), BF16),
        pltpu.VMEM((288, 256), BF16),
        pltpu.VMEM((144, 512), F32),
        pltpu.VMEM((128, LANES), BF16),
        pltpu.VMEM((384, LANES), BF16),
        pltpu.VMEM((ROWS, 2 * LANES), BF16),
        pltpu.VMEM((384, LANES), F32),
        pltpu.VMEM((48, FROWS), F32),
        pltpu.VMEM((4, LANES, LANES), F32),
        pltpu.VMEM((512, 512), BF16),
        pltpu.VMEM((512, 256), BF16),
        pltpu.VMEM((256, 512), BF16),
        pltpu.VMEM((2, 4, LANES), F32),
        pltpu.VMEM((QUANTITIES, QUANTITIES, 4, LANES), F32),
        pltpu.VMEM((SLOTS, 2, QUANTITIES * 8, LANES), F32),
        pltpu.VMEM((SLOTS, 2, QUANTITIES * 8, LANES), F32),
        pltpu.VMEM((SLOTS, 2, FAR_GROUPS * 8, LANES), F32),
        pltpu.VMEM((SLOTS, 2, FAR_GROUPS * 8, LANES), F32),
        pltpu.SemaphoreType.DMA((SLOTS, 4)),
        pltpu.SemaphoreType.DMA((SLOTS, 4)),
        pltpu.SemaphoreType.DMA((14,)),
    ]
    args = [pltpu.with_memory_space_constraint(arg, pltpu.HBM) for arg in args]
    return pl.pallas_call(
        functools.partial(kernel, devices),
        out_shape=jax.ShapeDtypeStruct(args[0].shape, F32),
        in_specs=[hbm] * len(args),
        out_specs=vmem,
        scratch_shapes=scratch,
        compiler_params=pltpu.CompilerParams(
            collective_id=0, has_side_effects=True, vmem_limit_bytes=40 * 2**20
        ),
    )(*args)


def solution(mesh):
    in_specs = (
        P(None, None, "dom"),
        P(None, None, None, "dom"),
        P(None, None, None, "dom"),
        P(None, None, None, "dom"),
        P(None, "dom"),
        P(None, "dom"),
        P(None, "dom"),
        P(None, "dom"),
        P("dom"),
        P(),
        P(),
        P(),
        P(),
        P(),
    )
    return jax.shard_map(
        functools.partial(body, mesh.shape["dom"]),
        mesh=mesh, in_specs=in_specs, out_specs=P(None, None, "dom"), check_vma=False,
    )
```

```python
import functools

import jax
import jax.numpy as jnp
from jax import lax
from jax.experimental import pallas as pl
from jax.experimental.pallas import tpu as pltpu
from jax.sharding import PartitionSpec as P

ELEM_DEV = 128
CAP_NEAR = 64
CAP_FAR = 32
QUANTITIES = 9
BASIS = 35
FACE_BASIS = 15
ORDER = 5
SLOTS = 4

LANES = 128
ROWS = 40
FROWS = 16
COLS = QUANTITIES * LANES
GROUPS = QUANTITIES * 2
FAR_GROUPS = 5
OFFSETS = (1, -1, 2, -2)
PARTS = ((range(0, 4), 0, 32, 0, 2), (range(4, 9), 32, 40, 16, 3))
BLOCKS = ((0, 1, 2, 3), (4, 5, 6, 7), (8,))
F32 = jnp.float32
BF16 = jnp.bfloat16
HIGHEST = lax.Precision.HIGHEST


def halves(value):
    high = value.astype(BF16).astype(F32)
    return high, value - high


def stacked(value):
    high, low = halves(value)
    tail = jnp.zeros((LANES - 3 * ROWS, value.shape[1]), F32)
    return jnp.concatenate([high, low, high, tail], axis=0).astype(BF16)


def widened(value):
    high, low = halves(value)
    return (high + pltpu.roll(high, ROWS, 1) + pltpu.roll(low, 2 * ROWS, 1)).astype(BF16)


def column_of(row):
    return jnp.broadcast_to(row, (LANES, LANES)).T


def dot(a, b):
    return jnp.dot(a, b, preferred_element_type=F32)


def kernel(devices, *refs):
    operands, out, landed, (
        fields, start, integral, rhs, first_z, second_z, turned_out, own_out, face_rhs, own_terms, spread, arrived, gathered,
        deriv_w, all_w, lift_w, pad_w, turn_w, tile_w,
        one_local, one_send, one_recv, where_from, flux_own,
        near_out, near_in, far_out, far_in, send_sem, recv_sem,
        in_sem,
    ) = refs[:14], refs[14], refs[15:29], refs[29:]
    (
        dofs, star, flux_local, flux_neigh, neighbour, neighbour_face, orientation, face_kind, cluster,
        deriv_stiff, update_stiff, face_proj, face_lift, orient_map,
    ) = landed
    loads = [
        pltpu.make_async_copy(operands[number], landed[number], in_sem.at[number])
        for number in range(14)
    ]
    first_loads = (9, 0, 1, 8, 4, 5, 7, 11, 13, 10, 6)
    late_loads = (12, 2, 3)
    for number in first_loads + late_loads:
        loads[number].start()

    me = lax.axis_index("dom")
    partners = [lax.rem(me + (off + devices), devices) for off in OFFSETS]
    barrier = pltpu.get_barrier_semaphore()
    for partner in partners:
        pl.semaphore_signal(
            barrier, inc=1, device_id=(partner,), device_id_type=pl.DeviceIdType.MESH
        )

    pad_w[...] = jnp.zeros_like(pad_w)
    turn_w[...] = jnp.zeros_like(turn_w)
    tile_w[...] = jnp.zeros_like(tile_w)
    deriv_w[...] = jnp.zeros_like(deriv_w)
    all_w[...] = jnp.zeros_like(all_w)
    fields[...] = jnp.zeros_like(fields)
    start[...] = jnp.zeros_like(start)
    face_rhs[...] = jnp.zeros_like(face_rhs)
    for number in first_loads:
        loads[number].wait()
    for d in range(3):
        pad_w[d * ROWS:d * ROWS + BASIS, 0:BASIS] = deriv_stiff[d]
        tile_w[d, 0:BASIS, 0:BASIS] = update_stiff[d]
    deriv_w[0:128, :] = widened(pad_w[0:128, :])
    for d in range(3):
        pad_w[256 + d * ROWS:256 + (d + 1) * ROWS, :] = tile_w[d].T[0:ROWS, :]
    for f in range(4):
        pad_w[192 + f * FROWS:192 + (f + 1) * FROWS, :] = jnp.zeros((FROWS, LANES), F32)
        pad_w[192 + f * FROWS:192 + f * FROWS + FACE_BASIS, 0:BASIS] = face_proj[:, f, :]
    for o in range(3):
        turn_w[o * FROWS:o * FROWS + FACE_BASIS, 0:FACE_BASIS] = orient_map[o]
    own_rows = jnp.concatenate(
        [pad_w[192 + f * FROWS:192 + (f + 1) * FROWS, :] for f in range(4)], axis=1
    )
    turned_rows = jnp.dot(turn_w[...], own_rows, precision=HIGHEST, preferred_element_type=F32)
    for f in range(4):
        pad_w[f * 48:(f + 1) * 48, :] = turned_rows[:, f * LANES:(f + 1) * LANES]
    all_w[...] = widened(pad_w[...])

    shape = (4, LANES)
    lane4 = lax.broadcasted_iota(jnp.int32, shape, 1)
    face4 = lax.broadcasted_iota(jnp.int32, shape, 0)
    nb = neighbour[...]
    nf = neighbour_face[...]
    kind = face_kind[...]
    local_id = nb & (ELEM_DEV - 1)
    distance = (nb >> 7) - me
    distance = jnp.where(distance < 0, distance + devices, distance)
    interior = kind == 0
    group = jnp.full(shape, 4, jnp.int32)
    for number, off in enumerate(OFFSETS):
        group = jnp.where(interior & (distance == off % devices), number, group)
    own_key = lane4 * 4 + face4
    far_key = local_id * 4 + nf
    key = jnp.where((group == 0) | (group == 2), own_key, far_key)
    low = (group * 1024).astype(F32)
    full_key = (group * 1024 + key).astype(F32)
    columns = [column_of(full_key[f:f + 1, :]) for f in range(4)]
    ranks = []
    for f in range(4):
        count = jnp.zeros((LANES, LANES), F32)
        for g in range(4):
            before = (columns[g] < full_key[f:f + 1, :]) & (columns[g] >= low[f:f + 1, :])
            count = count + jnp.where(before, 1.0, 0.0)
        ranks.append(jnp.sum(count, axis=0, keepdims=True))
    rank = jnp.concatenate(ranks, axis=0)
    base = jnp.where(group == 0, 0.0, jnp.where(group == 1, 64.0, jnp.where(group == 2, 128.0, 160.0)))
    place = jnp.where(group < 4, base + rank, -1.0)
    inside = interior & (distance == 0)
    source = jnp.where(inside, nf * LANES + local_id, -1).astype(F32)
    lane128 = lax.broadcasted_iota(jnp.int32, (LANES, LANES), 1).astype(F32)
    for f in range(4):
        cols = slice(f * LANES, (f + 1) * LANES)
        place_col = column_of(place[f:f + 1, :])
        one_send[cols, 0:LANES] = jnp.where(place_col == lane128, 1.0, 0.0).astype(BF16)
        one_send[cols, LANES:] = jnp.where(place_col == lane128 + 128.0, 1.0, 0.0).astype(BF16)
    where_from[0] = source
    where_from[1] = place

    def late_setup():
        for number in late_loads:
            loads[number].wait()
        row512 = lax.broadcasted_iota(jnp.int32, (4 * LANES, LANES), 0).astype(F32)
        row256 = row512[0:2 * LANES, :]
        for f in range(4):
            cols = slice(f * LANES, (f + 1) * LANES)
            one_local[:, cols] = jnp.where(row512 == where_from[0, f:f + 1, :], 1.0, 0.0).astype(BF16)
            one_recv[:, cols] = jnp.where(row256 == where_from[1, f:f + 1, :], 1.0, 0.0).astype(BF16)
        mirror = jnp.where(
            lax.broadcasted_iota(jnp.int32, (QUANTITIES, 4, LANES), 0) < 6, -1.0, 1.0
        ).astype(F32)
        factor = mirror * jnp.where(face_kind[...] == 1, 1.0, 0.0)[None]
        for q in range(QUANTITIES):
            flux_own[q] = flux_local[q] + factor * flux_neigh[q]
        for f in range(4):
            tile_w[3, f * FROWS:f * FROWS + FACE_BASIS, 0:BASIS] = face_lift[:, f, :]
        lift_high, lift_low = halves(tile_w[3].T[0:ROWS, :])
        lift_w[:, 0:LANES] = (lift_high + pltpu.roll(lift_high, 64, 1)).astype(BF16)
        lift_w[:, LANES:] = lift_low.astype(BF16)

    for q in range(QUANTITIES):
        fields[q, 0:BASIS, :] = dofs[q]

    span_low = jnp.left_shift(jnp.ones((1, LANES), jnp.int32), cluster[...]) - 1
    lane8 = lax.broadcasted_iota(jnp.int32, (8, LANES), 1)
    left = lane8 < 64
    quarter = lane8 // 32
    turned = [orientation[f:f + 1, :] for f in range(4)]

    def span_of(block):
        return slice(block[0] * LANES, (block[-1] + 1) * LANES)

    def col(q):
        return slice(q * LANES, (q + 1) * LANES)

    def contract(source_ref, row, block):
        totals = [None] * len(block)
        for p in range(QUANTITIES):
            for d in range(3):
                values = source_ref[row + d * ROWS:row + (d + 1) * ROWS, col(p)]
                for i, q in enumerate(block):
                    term = star[q, p, d:d + 1, :] * values
                    totals[i] = term if totals[i] is None else totals[i] + term
        return totals

    def face_contract(flux, source_ref, f, block, where):
        totals = [None] * len(block)
        for p in range(QUANTITIES):
            values = source_ref[where(f, p)]
            for i, q in enumerate(block):
                term = flux[q, p, f:f + 1, :] * values
                totals[i] = term if totals[i] is None else totals[i] + term
        return totals

    def send_part(slot, part, packed, copies):
        members, near_row, near_rows, far_row, groups = PARTS[part]
        first = 2 * members[0]
        count = 2 * len(members)
        for q in members:
            rows = slice(q * 8, (q + 1) * 8)
            even, odd = packed[q][0:8, 0:LANES], packed[q][8:16, 0:LANES]
            near_out[slot, 0, rows, :] = jnp.where(left, even, pltpu.roll(odd, 64, 1))
            near_out[slot, 1, rows, :] = jnp.where(left, pltpu.roll(even, 64, 1), odd)
        far = [packed[(first + i) // 2][(i % 2) * 8:(i % 2) * 8 + 8, LANES:] for i in range(count)]
        for j in range(groups):
            rows = slice(far_row + j * 8, far_row + (j + 1) * 8)
            for side in range(2):
                value = pltpu.roll(far[j], 96, 1) if side else far[j]
                for c in range(1, 4):
                    if j + groups * c < count:
                        shift = (32 * c - 32 * side) % LANES
                        piece = far[j + groups * c]
                        value = jnp.where(quarter == c, pltpu.roll(piece, shift, 1) if shift else piece, value)
                far_out[slot, side, rows, :] = value
        for number in range(4):
            here, there = (near_out, near_in) if number < 2 else (far_out, far_in)
            rows = pl.ds(near_row, near_rows) if number < 2 else pl.ds(far_row, groups * 8)
            copy = pltpu.make_async_remote_copy(
                src_ref=here.at[slot, number % 2, rows],
                dst_ref=there.at[slot, 1 - number % 2, rows],
                send_sem=send_sem.at[slot, part * 4 + number],
                recv_sem=recv_sem.at[slot, part * 4 + (number ^ 1)],
                device_id=(partners[number],),
                device_id_type=pl.DeviceIdType.MESH,
            )
            copy.start()
            copies.append(copy)

    def slot_step(slot, carry, first_slot=False):
        offset = span_low & slot
        below = offset.astype(F32)
        above = below + 1.0
        weights = []
        up, down = above, below
        scale = 1.0
        for degree in range(ORDER):
            scale = scale / (degree + 1)
            weights.append((up - down) * scale)
            up, down = up * above, down * below
        begins = offset == 0

        for block in BLOCKS:
            for q in block:
                first = fields[q] if first_slot else jnp.where(begins, fields[q], start[q])
                start[q] = first
                integral[q] = weights[0] * first
                rhs[:, col(q)] = stacked(first)
            first_z[:, span_of(block)] = dot(deriv_w[...], rhs[:, span_of(block)])

        packed = []
        copies = []
        for degree in range(1, ORDER):
            z_now, z_next = (first_z, second_z) if degree % 2 else (second_z, first_z)
            last = degree == ORDER - 1
            for block in BLOCKS:
                totals = contract(z_now, 0, block)
                for q, total in zip(block, totals):
                    term = -total
                    sum_now = integral[q] + weights[degree] * term
                    if last:
                        rhs[:, col(q)] = stacked(sum_now)
                    else:
                        integral[q] = sum_now
                        rhs[:, col(q)] = stacked(term)
                cols = span_of(block)
                if last:
                    turned_out[:, cols] = dot(all_w[0:192, :], rhs[:, cols])
                    for q in block:
                        for f in range(4):
                            r = f * 48
                            value = jnp.where(
                                turned[f] == 0, turned_out[r:r + 16, col(q)],
                                jnp.where(turned[f] == 1, turned_out[r + 16:r + 32, col(q)],
                                          turned_out[r + 32:r + 48, col(q)]),
                            )
                            high, lower = halves(value)
                            spread[q * 32:q * 32 + 16, col(f)] = high.astype(BF16)
                            spread[q * 32 + 16:q * 32 + 32, col(f)] = lower.astype(BF16)
                    piece = dot(spread[block[0] * 32:(block[-1] + 1) * 32, :], one_send[...])
                    for i in range(len(block)):
                        packed.append(piece[i * 32:i * 32 + 16, :] + piece[i * 32 + 16:i * 32 + 32, :])
                    if block[-1] == PARTS[0][0][-1]:
                        if first_slot:
                            pl.semaphore_wait(barrier, 4)
                        send_part(slot, 0, packed, copies)
                else:
                    z_next[:, cols] = dot(deriv_w[...], rhs[:, cols])

        send_part(slot, 1, packed, copies)

        if first_slot:
            late_setup()
        both = dot(spread[...], one_local[...])
        for q in range(QUANTITIES):
            gathered[q * 16:q * 16 + 16, :] = both[q * 32:q * 32 + 16, :] + both[q * 32 + 16:q * 32 + 32, :]
        for block in BLOCKS:
            own_out[:, span_of(block)] = dot(all_w[192:384, :], rhs[:, span_of(block)])
        for block in BLOCKS:
            totals = contract(own_out, 64, block)
            for q, total in zip(block, totals):
                fields[q] = fields[q] + total
        for f in range(4):
            for block in BLOCKS:
                totals = face_contract(
                    flux_own, own_out, f, block, lambda f, p: (slice(f * FROWS, (f + 1) * FROWS), col(p))
                )
                for q, total in zip(block, totals):
                    own_terms[f * FROWS:(f + 1) * FROWS, col(q)] = total

        for part, (members, near_row, near_rows, far_row, groups) in enumerate(PARTS):
            for number in range(4):
                copies[part * 4 + number].wait_recv()
            first = 2 * members[0]
            count = 2 * len(members)
            for q in members:
                rows = slice(q * 8, (q + 1) * 8)
                ahead, behind = near_in[slot, 0, rows, :], near_in[slot, 1, rows, :]
                even = jnp.where(left, ahead, pltpu.roll(behind, 64, 1))
                odd = jnp.where(left, pltpu.roll(ahead, 64, 1), behind)
                high, lower = halves(jnp.concatenate([even, odd], axis=0))
                arrived[q * 32:q * 32 + 16, 0:LANES] = high.astype(BF16)
                arrived[q * 32 + 16:q * 32 + 32, 0:LANES] = lower.astype(BF16)
            pieces = [None] * count
            for j in range(groups):
                rows = slice(far_row + j * 8, far_row + (j + 1) * 8)
                ahead, behind = far_in[slot, 0, rows, :], far_in[slot, 1, rows, :]
                for c in range(4):
                    if j + groups * c < count:
                        near_side = pltpu.roll(ahead, (-32 * c) % LANES, 1) if c else ahead
                        shift = (32 - 32 * c) % LANES
                        far_side = pltpu.roll(behind, shift, 1) if shift else behind
                        pieces[j + groups * c] = jnp.where(quarter == 0, near_side, far_side)
            for i, q in enumerate(members):
                high, lower = halves(jnp.concatenate([pieces[2 * i], pieces[2 * i + 1]], axis=0))
                arrived[q * 32:q * 32 + 16, LANES:] = high.astype(BF16)
                arrived[q * 32 + 16:q * 32 + 32, LANES:] = lower.astype(BF16)
            both = dot(arrived[members[0] * 32:(members[-1] + 1) * 32, :], one_recv[...])
            for i, q in enumerate(members):
                gathered[q * 16:(q + 1) * 16, :] = gathered[q * 16:(q + 1) * 16, :] + (
                    both[i * 32:i * 32 + 16, :] + both[i * 32 + 16:i * 32 + 32, :]
                )
        for block in BLOCKS:
            cols = span_of(block)
            for f in range(4):
                totals = face_contract(
                    flux_neigh, gathered, f, block, lambda f, p: (slice(p * FROWS, (p + 1) * FROWS), col(f))
                )
                for q, total in zip(block, totals):
                    row = f * FROWS
                    high, lower = halves(own_terms[row:row + FROWS, col(q)] + total)
                    high = high.astype(BF16)
                    face_rhs[row:row + FROWS, col(q)] = high
                    face_rhs[row + 64:row + 64 + FROWS, col(q)] = lower.astype(BF16)
                    face_rhs[row + 128:row + 128 + FROWS, col(q)] = high
            lifted = dot(lift_w[...], face_rhs[:, cols])
            for i, q in enumerate(block):
                fields[q] = fields[q] - lifted[0:ROWS, col(i)]
        for copy in copies:
            copy.wait_send()
        return carry

    slot_step(0, 0, first_slot=True)
    lax.fori_loop(1, SLOTS, slot_step, 0)
    for q in range(QUANTITIES):
        out[q] = fields[q, 0:BASIS, :]


def body(devices, *args):
    args = list(args)
    args[8] = args[8].reshape(1, -1)
    for number in (1, 2, 3):
        args[number] = jnp.transpose(args[number], (1, 2, 0, 3))
    args[11] = jnp.transpose(args[11], (1, 0, 2))
    args[12] = jnp.transpose(args[12], (2, 0, 1))
    vmem = pl.BlockSpec(memory_space=pltpu.VMEM)
    hbm = pl.BlockSpec(memory_space=pltpu.HBM)
    scratch = [pltpu.VMEM(arg.shape, arg.dtype) for arg in args] + [
        pltpu.VMEM((QUANTITIES, ROWS, LANES), F32),
        pltpu.VMEM((QUANTITIES, ROWS, LANES), F32),
        pltpu.VMEM((QUANTITIES, ROWS, LANES), F32),
        pltpu.VMEM((LANES, COLS), BF16),
        pltpu.VMEM((128, COLS), F32),
        pltpu.VMEM((128, COLS), F32),
        pltpu.VMEM((192, COLS), F32),
        pltpu.VMEM((192, COLS), F32),
        pltpu.VMEM((256, COLS), BF16),
        pltpu.VMEM((4 * FROWS, COLS), F32),
        pltpu.VMEM((288, 512), BF16),
        pltpu.VMEM((288, 256), BF16),
        pltpu.VMEM((144, 512), F32),
        pltpu.VMEM((128, LANES), BF16),
        pltpu.VMEM((384, LANES), BF16),
        pltpu.VMEM((ROWS, 2 * LANES), BF16),
        pltpu.VMEM((384, LANES), F32),
        pltpu.VMEM((48, FROWS), F32),
        pltpu.VMEM((4, LANES, LANES), F32),
        pltpu.VMEM((512, 512), BF16),
        pltpu.VMEM((512, 256), BF16),
        pltpu.VMEM((256, 512), BF16),
        pltpu.VMEM((2, 4, LANES), F32),
        pltpu.VMEM((QUANTITIES, QUANTITIES, 4, LANES), F32),
        pltpu.VMEM((SLOTS, 2, QUANTITIES * 8, LANES), F32),
        pltpu.VMEM((SLOTS, 2, QUANTITIES * 8, LANES), F32),
        pltpu.VMEM((SLOTS, 2, FAR_GROUPS * 8, LANES), F32),
        pltpu.VMEM((SLOTS, 2, FAR_GROUPS * 8, LANES), F32),
        pltpu.SemaphoreType.DMA((SLOTS, 8)),
        pltpu.SemaphoreType.DMA((SLOTS, 8)),
        pltpu.SemaphoreType.DMA((14,)),
    ]
    args = [pltpu.with_memory_space_constraint(arg, pltpu.HBM) for arg in args]
    return pl.pallas_call(
        functools.partial(kernel, devices),
        out_shape=jax.ShapeDtypeStruct(args[0].shape, F32),
        in_specs=[hbm] * len(args),
        out_specs=vmem,
        scratch_shapes=scratch,
        compiler_params=pltpu.CompilerParams(
            collective_id=0, has_side_effects=True, vmem_limit_bytes=40 * 2**20
        ),
    )(*args)


def solution(mesh):
    in_specs = (
        P(None, None, "dom"),
        P(None, None, None, "dom"),
        P(None, None, None, "dom"),
        P(None, None, None, "dom"),
        P(None, "dom"),
        P(None, "dom"),
        P(None, "dom"),
        P(None, "dom"),
        P("dom"),
        P(),
        P(),
        P(),
        P(),
        P(),
    )
    return jax.shard_map(
        functools.partial(body, mesh.shape["dom"]),
        mesh=mesh, in_specs=in_specs, out_specs=P(None, None, "dom"), check_vma=False,
    )
```

```python
import functools

import jax
import jax.numpy as jnp
from jax import lax
from jax.experimental import pallas as pl
from jax.experimental.pallas import tpu as pltpu
from jax.sharding import PartitionSpec as P

ELEM_DEV = 128
CAP_NEAR = 64
CAP_FAR = 32
QUANTITIES = 9
BASIS = 35
FACE_BASIS = 15
ORDER = 5
SLOTS = 4

LANES = 128
ROWS = 40
FROWS = 16
COLS = QUANTITIES * LANES
GROUPS = QUANTITIES * 2
FAR_GROUPS = 5
OFFSETS = (1, -1, 2, -2)
BLOCKS = ((0, 1, 2, 3), (4, 5, 6, 7), (8,))
F32 = jnp.float32
BF16 = jnp.bfloat16
HIGHEST = lax.Precision.HIGHEST


def halves(value):
    high = value.astype(BF16).astype(F32)
    return high, value - high


def stacked(value):
    high, low = halves(value)
    tail = jnp.zeros((LANES - 3 * ROWS, value.shape[1]), F32)
    return jnp.concatenate([high, low, high, tail], axis=0).astype(BF16)


def widened(value):
    high, low = halves(value)
    return (high + pltpu.roll(high, ROWS, 1) + pltpu.roll(low, 2 * ROWS, 1)).astype(BF16)


def column_of(row):
    return jnp.broadcast_to(row, (LANES, LANES)).T


def dot(a, b):
    return jnp.dot(a, b, preferred_element_type=F32)


def kernel(devices, *refs):
    operands, out, landed, (
        fields, start, integral, rhs, first_z, second_z, turned_out, own_out, face_rhs, own_terms, spread, arrived, gathered,
        deriv_w, all_w, lift_w, pad_w, turn_w, tile_w,
        one_local, one_send, one_recv, where_from, flux_own,
        near_out, near_in, far_out, far_in, send_sem, recv_sem,
        in_sem,
    ) = refs[:14], refs[14], refs[15:29], refs[29:]
    (
        dofs, star, flux_local, flux_neigh, neighbour, neighbour_face, orientation, face_kind, cluster,
        deriv_stiff, update_stiff, face_proj, face_lift, orient_map,
    ) = landed
    loads = [
        pltpu.make_async_copy(operands[number], landed[number], in_sem.at[number])
        for number in range(14)
    ]
    first_loads = (9, 0, 1, 8, 4, 5, 7, 11, 13, 10, 6)
    late_loads = (12, 2, 3)
    for number in first_loads + late_loads:
        loads[number].start()

    me = lax.axis_index("dom")
    partners = [lax.rem(me + (off + devices), devices) for off in OFFSETS]
    barrier = pltpu.get_barrier_semaphore()
    for partner in partners:
        pl.semaphore_signal(
            barrier, inc=1, device_id=(partner,), device_id_type=pl.DeviceIdType.MESH
        )

    pad_w[...] = jnp.zeros_like(pad_w)
    turn_w[...] = jnp.zeros_like(turn_w)
    tile_w[...] = jnp.zeros_like(tile_w)
    deriv_w[...] = jnp.zeros_like(deriv_w)
    all_w[...] = jnp.zeros_like(all_w)
    fields[...] = jnp.zeros_like(fields)
    start[...] = jnp.zeros_like(start)
    face_rhs[...] = jnp.zeros_like(face_rhs)
    for number in first_loads:
        loads[number].wait()
    for d in range(3):
        pad_w[d * ROWS:d * ROWS + BASIS, 0:BASIS] = deriv_stiff[d]
        tile_w[d, 0:BASIS, 0:BASIS] = update_stiff[d]
    deriv_w[0:128, :] = widened(pad_w[0:128, :])
    for d in range(3):
        pad_w[256 + d * ROWS:256 + (d + 1) * ROWS, :] = tile_w[d].T[0:ROWS, :]
    for f in range(4):
        pad_w[192 + f * FROWS:192 + (f + 1) * FROWS, :] = jnp.zeros((FROWS, LANES), F32)
        pad_w[192 + f * FROWS:192 + f * FROWS + FACE_BASIS, 0:BASIS] = face_proj[:, f, :]
    for o in range(3):
        turn_w[o * FROWS:o * FROWS + FACE_BASIS, 0:FACE_BASIS] = orient_map[o]
    own_rows = jnp.concatenate(
        [pad_w[192 + f * FROWS:192 + (f + 1) * FROWS, :] for f in range(4)], axis=1
    )
    turned_rows = jnp.dot(turn_w[...], own_rows, precision=HIGHEST, preferred_element_type=F32)
    for f in range(4):
        pad_w[f * 48:(f + 1) * 48, :] = turned_rows[:, f * LANES:(f + 1) * LANES]
    all_w[...] = widened(pad_w[...])

    shape = (4, LANES)
    lane4 = lax.broadcasted_iota(jnp.int32, shape, 1)
    face4 = lax.broadcasted_iota(jnp.int32, shape, 0)
    nb = neighbour[...]
    nf = neighbour_face[...]
    kind = face_kind[...]
    local_id = nb & (ELEM_DEV - 1)
    distance = (nb >> 7) - me
    distance = jnp.where(distance < 0, distance + devices, distance)
    interior = kind == 0
    group = jnp.full(shape, 4, jnp.int32)
    for number, off in enumerate(OFFSETS):
        group = jnp.where(interior & (distance == off % devices), number, group)
    own_key = lane4 * 4 + face4
    far_key = local_id * 4 + nf
    key = jnp.where((group == 0) | (group == 2), own_key, far_key)
    low = (group * 1024).astype(F32)
    full_key = (group * 1024 + key).astype(F32)
    columns = [column_of(full_key[f:f + 1, :]) for f in range(4)]
    ranks = []
    for f in range(4):
        count = jnp.zeros((LANES, LANES), F32)
        for g in range(4):
            before = (columns[g] < full_key[f:f + 1, :]) & (columns[g] >= low[f:f + 1, :])
            count = count + jnp.where(before, 1.0, 0.0)
        ranks.append(jnp.sum(count, axis=0, keepdims=True))
    rank = jnp.concatenate(ranks, axis=0)
    base = jnp.where(group == 0, 0.0, jnp.where(group == 1, 64.0, jnp.where(group == 2, 128.0, 160.0)))
    place = jnp.where(group < 4, base + rank, -1.0)
    inside = interior & (distance == 0)
    source = jnp.where(inside, nf * LANES + local_id, -1).astype(F32)
    lane128 = lax.broadcasted_iota(jnp.int32, (LANES, LANES), 1).astype(F32)
    for f in range(4):
        cols = slice(f * LANES, (f + 1) * LANES)
        place_col = column_of(place[f:f + 1, :])
        one_send[cols, 0:LANES] = jnp.where(place_col == lane128, 1.0, 0.0).astype(BF16)
        one_send[cols, LANES:] = jnp.where(place_col == lane128 + 128.0, 1.0, 0.0).astype(BF16)
    where_from[0] = source
    where_from[1] = place

    def late_setup():
        for number in late_loads:
            loads[number].wait()
        row512 = lax.broadcasted_iota(jnp.int32, (4 * LANES, LANES), 0).astype(F32)
        row256 = row512[0:2 * LANES, :]
        for f in range(4):
            cols = slice(f * LANES, (f + 1) * LANES)
            one_local[:, cols] = jnp.where(row512 == where_from[0, f:f + 1, :], 1.0, 0.0).astype(BF16)
            one_recv[:, cols] = jnp.where(row256 == where_from[1, f:f + 1, :], 1.0, 0.0).astype(BF16)
        mirror = jnp.where(
            lax.broadcasted_iota(jnp.int32, (QUANTITIES, 4, LANES), 0) < 6, -1.0, 1.0
        ).astype(F32)
        factor = mirror * jnp.where(face_kind[...] == 1, 1.0, 0.0)[None]
        for q in range(QUANTITIES):
            flux_own[q] = flux_local[q] + factor * flux_neigh[q]
        for f in range(4):
            tile_w[3, f * FROWS:f * FROWS + FACE_BASIS, 0:BASIS] = face_lift[:, f, :]
        lift_high, lift_low = halves(tile_w[3].T[0:ROWS, :])
        lift_w[:, 0:LANES] = (lift_high + pltpu.roll(lift_high, 64, 1)).astype(BF16)
        lift_w[:, LANES:] = lift_low.astype(BF16)

    for q in range(QUANTITIES):
        fields[q, 0:BASIS, :] = dofs[q]

    span_low = jnp.left_shift(jnp.ones((1, LANES), jnp.int32), cluster[...]) - 1
    lane8 = lax.broadcasted_iota(jnp.int32, (8, LANES), 1)
    left = lane8 < 64
    quarter = lane8 // 32
    turned = [orientation[f:f + 1, :] for f in range(4)]

    def span_of(block):
        return slice(block[0] * LANES, (block[-1] + 1) * LANES)

    def col(q):
        return slice(q * LANES, (q + 1) * LANES)

    def contract(source_ref, row, block):
        totals = [None] * len(block)
        for p in range(QUANTITIES):
            for d in range(3):
                values = source_ref[row + d * ROWS:row + (d + 1) * ROWS, col(p)]
                for i, q in enumerate(block):
                    term = star[q, p, d:d + 1, :] * values
                    totals[i] = term if totals[i] is None else totals[i] + term
        return totals

    def face_contract(flux, source_ref, f, block, where):
        totals = [None] * len(block)
        for p in range(QUANTITIES):
            values = source_ref[where(f, p)]
            for i, q in enumerate(block):
                term = flux[q, p, f:f + 1, :] * values
                totals[i] = term if totals[i] is None else totals[i] + term
        return totals

    started = []

    def slot_step(slot, carry, first_slot=False):
        offset = span_low & slot
        below = offset.astype(F32)
        above = below + 1.0
        weights = []
        up, down = above, below
        scale = 1.0
        for degree in range(ORDER):
            scale = scale / (degree + 1)
            weights.append((up - down) * scale)
            up, down = up * above, down * below
        begins = offset == 0

        for block in BLOCKS:
            for q in block:
                first = fields[q] if first_slot else jnp.where(begins, fields[q], start[q])
                start[q] = first
                integral[q] = weights[0] * first
                rhs[:, col(q)] = stacked(first)
            first_z[:, span_of(block)] = dot(deriv_w[...], rhs[:, span_of(block)])

        packed = []
        for degree in range(1, ORDER):
            z_now, z_next = (first_z, second_z) if degree % 2 else (second_z, first_z)
            last = degree == ORDER - 1
            for block in BLOCKS:
                totals = contract(z_now, 0, block)
                for q, total in zip(block, totals):
                    term = -total
                    sum_now = integral[q] + weights[degree] * term
                    if last:
                        rhs[:, col(q)] = stacked(sum_now)
                    else:
                        integral[q] = sum_now
                        rhs[:, col(q)] = stacked(term)
                cols = span_of(block)
                if last:
                    turned_out[:, cols] = dot(all_w[0:192, :], rhs[:, cols])
                    for q in block:
                        for f in range(4):
                            r = f * 48
                            value = jnp.where(
                                turned[f] == 0, turned_out[r:r + 16, col(q)],
                                jnp.where(turned[f] == 1, turned_out[r + 16:r + 32, col(q)],
                                          turned_out[r + 32:r + 48, col(q)]),
                            )
                            high, lower = halves(value)
                            spread[q * 32:q * 32 + 16, col(f)] = high.astype(BF16)
                            spread[q * 32 + 16:q * 32 + 32, col(f)] = lower.astype(BF16)
                    piece = dot(spread[block[0] * 32:(block[-1] + 1) * 32, :], one_send[...])
                    for i in range(len(block)):
                        packed.append(piece[i * 32:i * 32 + 16, :] + piece[i * 32 + 16:i * 32 + 32, :])
                else:
                    z_next[:, cols] = dot(deriv_w[...], rhs[:, cols])

        packed = jnp.concatenate(packed, axis=0)
        near = [packed[r * 8:(r + 1) * 8, 0:LANES] for r in range(GROUPS)]
        far = [packed[r * 8:(r + 1) * 8, LANES:] for r in range(GROUPS)]
        for j in range(QUANTITIES):
            rows = slice(j * 8, (j + 1) * 8)
            near_out[slot, 0, rows, :] = jnp.where(left, near[2 * j], pltpu.roll(near[2 * j + 1], 64, 1))
            near_out[slot, 1, rows, :] = jnp.where(left, pltpu.roll(near[2 * j], 64, 1), near[2 * j + 1])
        for j in range(FAR_GROUPS):
            rows = slice(j * 8, (j + 1) * 8)
            for side in range(2):
                value = pltpu.roll(far[j], (-32 * side) % LANES, 1) if side else far[j]
                for c in range(1, 4):
                    r = j + FAR_GROUPS * c
                    if r < GROUPS:
                        shift = (32 * c - 32 * side) % LANES
                        moved = pltpu.roll(far[r], shift, 1) if shift else far[r]
                        value = jnp.where(quarter == c, moved, value)
                far_out[slot, side, rows, :] = value

        if first_slot:
            pl.semaphore_wait(barrier, 4)
        copies = []
        for number in range(4):
            here, there = (near_out, near_in) if number < 2 else (far_out, far_in)
            copies.append(pltpu.make_async_remote_copy(
                src_ref=here.at[slot, number % 2],
                dst_ref=there.at[slot, 1 - number % 2],
                send_sem=send_sem.at[slot, number],
                recv_sem=recv_sem.at[slot, number ^ 1],
                device_id=(partners[number],),
                device_id_type=pl.DeviceIdType.MESH,
            ))
        for copy in copies:
            copy.start()

        if first_slot:
            late_setup()
        both = dot(spread[...], one_local[...])
        for q in range(QUANTITIES):
            gathered[q * 16:q * 16 + 16, :] = both[q * 32:q * 32 + 16, :] + both[q * 32 + 16:q * 32 + 32, :]
        for block in BLOCKS:
            own_out[:, span_of(block)] = dot(all_w[192:384, :], rhs[:, span_of(block)])
        for block in BLOCKS:
            totals = contract(own_out, 64, block)
            for q, total in zip(block, totals):
                fields[q] = fields[q] + total
        for f in range(4):
            for block in BLOCKS:
                totals = face_contract(
                    flux_own, own_out, f, block, lambda f, p: (slice(f * FROWS, (f + 1) * FROWS), col(p))
                )
                for q, total in zip(block, totals):
                    own_terms[f * FROWS:(f + 1) * FROWS, col(q)] = total

        for number in range(4):
            copies[number].wait_recv()
        for j in range(QUANTITIES):
            rows = slice(j * 8, (j + 1) * 8)
            ahead, behind = near_in[slot, 0, rows, :], near_in[slot, 1, rows, :]
            even = jnp.where(left, ahead, pltpu.roll(behind, 64, 1))
            odd = jnp.where(left, pltpu.roll(ahead, 64, 1), behind)
            high, lower = halves(jnp.concatenate([even, odd], axis=0))
            arrived[j * 16:(j + 1) * 16, 0:LANES] = high.astype(BF16)
            arrived[144 + j * 16:144 + (j + 1) * 16, 0:LANES] = lower.astype(BF16)
        pieces = [None] * GROUPS
        for j in range(FAR_GROUPS):
            rows = slice(j * 8, (j + 1) * 8)
            ahead, behind = far_in[slot, 0, rows, :], far_in[slot, 1, rows, :]
            for c in range(4):
                r = j + FAR_GROUPS * c
                if r < GROUPS:
                    first = pltpu.roll(ahead, (-32 * c) % LANES, 1) if c else ahead
                    shift = (32 - 32 * c) % LANES
                    second = pltpu.roll(behind, shift, 1) if shift else behind
                    pieces[r] = jnp.where(quarter == 0, first, second)
        for j in range(QUANTITIES):
            high, lower = halves(jnp.concatenate([pieces[2 * j], pieces[2 * j + 1]], axis=0))
            arrived[j * 16:(j + 1) * 16, LANES:] = high.astype(BF16)
            arrived[144 + j * 16:144 + (j + 1) * 16, LANES:] = lower.astype(BF16)
        both = dot(arrived[...], one_recv[...])
        gathered[...] = gathered[...] + (both[0:144, :] + both[144:288, :])

        for block in BLOCKS:
            cols = span_of(block)
            for f in range(4):
                totals = face_contract(
                    flux_neigh, gathered, f, block, lambda f, p: (slice(p * FROWS, (p + 1) * FROWS), col(f))
                )
                for q, total in zip(block, totals):
                    row = f * FROWS
                    high, lower = halves(own_terms[row:row + FROWS, col(q)] + total)
                    high = high.astype(BF16)
                    face_rhs[row:row + FROWS, col(q)] = high
                    face_rhs[row + 64:row + 64 + FROWS, col(q)] = lower.astype(BF16)
                    face_rhs[row + 128:row + 128 + FROWS, col(q)] = high
            lifted = dot(lift_w[...], face_rhs[:, cols])
            for i, q in enumerate(block):
                fields[q] = fields[q] - lifted[0:ROWS, col(i)]
        started.extend(copies)
        return carry

    for slot in range(SLOTS):
        slot_step(slot, 0, first_slot=slot == 0)
    for copy in started:
        copy.wait_send()
    for q in range(QUANTITIES):
        out[q] = fields[q, 0:BASIS, :]


def body(devices, *args):
    args = list(args)
    args[8] = args[8].reshape(1, -1)
    for number in (1, 2, 3):
        args[number] = jnp.transpose(args[number], (1, 2, 0, 3))
    args[11] = jnp.transpose(args[11], (1, 0, 2))
    args[12] = jnp.transpose(args[12], (2, 0, 1))
    vmem = pl.BlockSpec(memory_space=pltpu.VMEM)
    hbm = pl.BlockSpec(memory_space=pltpu.HBM)
    scratch = [pltpu.VMEM(arg.shape, arg.dtype) for arg in args] + [
        pltpu.VMEM((QUANTITIES, ROWS, LANES), F32),
        pltpu.VMEM((QUANTITIES, ROWS, LANES), F32),
        pltpu.VMEM((QUANTITIES, ROWS, LANES), F32),
        pltpu.VMEM((LANES, COLS), BF16),
        pltpu.VMEM((128, COLS), F32),
        pltpu.VMEM((128, COLS), F32),
        pltpu.VMEM((192, COLS), F32),
        pltpu.VMEM((192, COLS), F32),
        pltpu.VMEM((256, COLS), BF16),
        pltpu.VMEM((4 * FROWS, COLS), F32),
        pltpu.VMEM((288, 512), BF16),
        pltpu.VMEM((288, 256), BF16),
        pltpu.VMEM((144, 512), F32),
        pltpu.VMEM((128, LANES), BF16),
        pltpu.VMEM((384, LANES), BF16),
        pltpu.VMEM((ROWS, 2 * LANES), BF16),
        pltpu.VMEM((384, LANES), F32),
        pltpu.VMEM((48, FROWS), F32),
        pltpu.VMEM((4, LANES, LANES), F32),
        pltpu.VMEM((512, 512), BF16),
        pltpu.VMEM((512, 256), BF16),
        pltpu.VMEM((256, 512), BF16),
        pltpu.VMEM((2, 4, LANES), F32),
        pltpu.VMEM((QUANTITIES, QUANTITIES, 4, LANES), F32),
        pltpu.VMEM((SLOTS, 2, QUANTITIES * 8, LANES), F32),
        pltpu.VMEM((SLOTS, 2, QUANTITIES * 8, LANES), F32),
        pltpu.VMEM((SLOTS, 2, FAR_GROUPS * 8, LANES), F32),
        pltpu.VMEM((SLOTS, 2, FAR_GROUPS * 8, LANES), F32),
        pltpu.SemaphoreType.DMA((SLOTS, 4)),
        pltpu.SemaphoreType.DMA((SLOTS, 4)),
        pltpu.SemaphoreType.DMA((14,)),
    ]
    args = [pltpu.with_memory_space_constraint(arg, pltpu.HBM) for arg in args]
    return pl.pallas_call(
        functools.partial(kernel, devices),
        out_shape=jax.ShapeDtypeStruct(args[0].shape, F32),
        in_specs=[hbm] * len(args),
        out_specs=vmem,
        scratch_shapes=scratch,
        compiler_params=pltpu.CompilerParams(
            collective_id=0, has_side_effects=True, vmem_limit_bytes=40 * 2**20
        ),
    )(*args)


def solution(mesh):
    in_specs = (
        P(None, None, "dom"),
        P(None, None, None, "dom"),
        P(None, None, None, "dom"),
        P(None, None, None, "dom"),
        P(None, "dom"),
        P(None, "dom"),
        P(None, "dom"),
        P(None, "dom"),
        P("dom"),
        P(),
        P(),
        P(),
        P(),
        P(),
    )
    return jax.shard_map(
        functools.partial(body, mesh.shape["dom"]),
        mesh=mesh, in_specs=in_specs, out_specs=P(None, None, "dom"), check_vma=False,
    )
```
